512 devices in a mesh: context: 32 (over y, z_lo, core), tensor: 16 (over x, z_hi).
Axes of the slice: x: 4, y: 4, z: 16 (z_hi: 4, z_lo: 4; z = z_hi * 4 + z_lo), core: 2. Of those that a mesh axis runs over, the one named last changes fastest.
Arguments:
- tokens: bfloat16 [8192, 4096], P(('context', 'tensor')), may hold values from -6 to 6
- x_weight: bfloat16 [4096, 8192], P('context', 'tensor'), may hold values from -0.09375 to 0.09375
- dt_weight: bfloat16 [4096, 128], P('context', 'tensor'), may hold values from -0.09375 to 0.09375
- bc_weight: bfloat16 [8, 4096, 256], P(None, 'context'), may hold values from -0.01953125 to 0.01953125
- conv_x: bfloat16 [4, 8192], P(None, 'tensor'), may hold values from -3 to 3
- conv_bc: bfloat16 [8, 4, 256], replicated, may hold values from -3 to 3
- dt_bias: float32 [128], P('tensor'), may hold values from -1.5 to 0.5
- a_rate: float32 [128], P('tensor'), may hold values from 2.4414063e-05 to 0.08
- d_skip: float32 [128], P('tensor'), may hold values from 0.5 to 1.5
- norm_gain: float32 [8192], P('tensor'), may hold values from 0.1 to 1.9
Outputs:
- normed_out: bfloat16 [8192, 8192], P('context', 'tensor')
The draws below stay inside these ranges and needn't reach their ends.
All inputs are finite; a program needn't handle non-finite values.
Results may differ from the reference program's by a relative error of at most 0.0085.
Values may be sent and summed in bfloat16 or wider, within the bound.
A program may use at most 64 MiB of HBM per device.

```python
import math
import jax
import jax.numpy as jnp
from jax import lax

D = 4096
HEADS = 128
HEAD_DIM = 64
STATE = 128
GROUPS = 8
SPAN = 256
CONV = 4
TOKENS = 8192


def draw_a_rate(key, part):
    key = jax.random.fold_in(key, 7)
    key_order, key_slow, key_fast = jax.random.split(key, 3)
    order = jax.random.permutation(key_order, HEADS)
    slow_mask = order < HEADS // 2
    slow_rate = jnp.exp(jax.random.uniform(key_slow, (HEADS,), jnp.float32, math.log(0.2), math.log(1.5))) / TOKENS
    fast_rate = jnp.exp(jax.random.uniform(key_fast, (HEADS,), jnp.float32, math.log(0.01), math.log(0.08)))
    return jnp.where(slow_mask, slow_rate, fast_rate).astype(jnp.float32)


def block_levels(own_key, extent, cuts, low, largest):
    def one(position, blocks):
        heights = jax.random.uniform(jax.random.fold_in(jax.random.fold_in(own_key, 6), position), (blocks,), jnp.float32, low / len(cuts), largest / len(cuts))
        return jnp.repeat(jnp.exp(heights), extent[position] // blocks).reshape((-1,) + (1,) * (len(extent) - position - 1))

    factor_of = one(*cuts[0])
    for cut in cuts[1:]:
        factor_of = factor_of * one(*cut)
    return factor_of


def gaussian(stream_key, extent, scale, most, pieces=(), held_as=jnp.bfloat16):
    array = jax.random.normal(stream_key, extent, jnp.float32) * scale
    if len(pieces) > 0:
        array = block_levels(stream_key, extent, pieces, -0.22, 0.18) * array
    return jnp.clip(array, min=-most, max=most).astype(held_as)


def setup_inputs(seed: int = 0) -> dict:
    keys = jax.random.split(jax.random.key(seed), 11)
    tokens = gaussian(keys[0], (TOKENS, D), 1.0, 6.0, ((0, 512),))
    x_weight = gaussian(keys[1], (D, HEADS * HEAD_DIM), D ** -0.5, 0.09375, ((0, 32), (1, 16)))
    dt_weight = gaussian(keys[2], (D, HEADS), D ** -0.5, 0.09375, ((0, 32), (1, 16)))
    bc_weight = gaussian(keys[3], (GROUPS, D, 2 * STATE), (25 * D) ** -0.5, 0.01953125, ((1, 32),))
    conv_x = gaussian(keys[4], (CONV, HEADS * HEAD_DIM), CONV ** -0.5, 3.0, ((1, 16),))
    conv_bc = gaussian(keys[5], (GROUPS, CONV, 2 * STATE), CONV ** -0.5, 3.0)
    dt_bias = jnp.clip(-1.5 + 2.0 * jax.random.uniform(keys[6], (HEADS,), jnp.float32) ** block_levels(keys[6], (HEADS,), ((0, 16),), -0.2, 0.2), -1.5, 0.5)
    a_rate = draw_a_rate(jax.random.fold_in(keys[10], 71), 0)
    d_skip = jnp.clip(0.5 + 1.0 * jax.random.uniform(keys[8], (HEADS,), jnp.float32) ** block_levels(keys[8], (HEADS,), ((0, 16),), -0.2, 0.2), 0.5, 1.5)
    norm_gain = jnp.clip(1.0 + 0.18 * jax.random.normal(keys[9], (HEADS * HEAD_DIM,), jnp.float32), 0.1, 1.9)
    return dict(tokens=tokens, x_weight=x_weight, dt_weight=dt_weight, bc_weight=bc_weight, conv_x=conv_x, conv_bc=conv_bc, dt_bias=dt_bias, a_rate=a_rate, d_skip=d_skip, norm_gain=norm_gain)


def causal_conv(values, taps):
    count = values.shape[0]
    padded = jnp.concatenate([jnp.zeros((CONV - 1, values.shape[1]), values.dtype), values], 0).astype(jnp.float32)
    total = jnp.zeros(values.shape, jnp.float32)
    for offset in range(CONV):
        total = total + taps[offset].astype(jnp.float32) * padded[offset:offset + count]
    return jax.nn.silu(total).astype(jnp.bfloat16)

def span_pieces(values, key_query, log_sums, step_sizes):
    length, heads_n, head_width = values.shape
    groups_n = key_query.shape[1]
    per_group = heads_n // groups_n
    inputs_b = key_query[:, :, 0].astype(jnp.float32)
    outputs_c = key_query[:, :, 1].astype(jnp.float32)
    scores = jnp.einsum('tgn,sgn->gts', outputs_c, inputs_b, precision=lax.Precision.HIGHEST)
    positions = jnp.arange(length)
    causal_mask = positions[:, None] >= positions[None, :]
    log_gaps = log_sums.T[:, :, None] - log_sums.T[:, None, :]
    decay_table = jnp.where(causal_mask, jnp.exp(jnp.where(causal_mask, log_gaps, 0.0)), 0.0)
    mixing = (scores[:, None] * decay_table.reshape(groups_n, per_group, length, length) * step_sizes.T.reshape(groups_n, per_group, 1, length)).astype(jnp.bfloat16)
    grouped = values.reshape(length, groups_n, per_group, head_width).astype(jnp.float32)
    inner_terms = jnp.einsum('gjts,sgjp->tgjp', mixing.astype(jnp.float32), grouped, precision=lax.Precision.HIGHEST).reshape(length, heads_n, head_width)
    tail_weight = jnp.exp(log_sums[-1][None, :] - log_sums) * step_sizes
    weighted = values.astype(jnp.float32) * tail_weight[:, :, None]
    states = jnp.einsum('sgjp,sgn->gjpn', weighted.reshape(length, groups_n, per_group, head_width), inputs_b, precision=lax.Precision.HIGHEST).reshape(heads_n, head_width, inputs_b.shape[2])
    return (inner_terms, states)

def span_reads(outputs_c, log_sums, start_state):
    length, groups_n, state_width = outputs_c.shape
    heads_n, head_width = (start_state.shape[0], start_state.shape[1])
    per_group = heads_n // groups_n
    reads = jnp.einsum('tgn,gjpn->tgjp', outputs_c.astype(jnp.float32), start_state.reshape(groups_n, per_group, head_width, state_width), precision=lax.Precision.HIGHEST)
    return reads.reshape(length, heads_n, head_width) * jnp.exp(log_sums)[:, :, None]

def finish(mixed, norm_gain):
    mean_square = lax.optimization_barrier(jnp.mean(mixed * mixed, axis=-1, keepdims=True))
    normed = mixed * lax.rsqrt(mean_square + 1e-05) * norm_gain.reshape(mixed.shape[1], mixed.shape[2]).astype(jnp.float32)
    return normed.astype(jnp.bfloat16).reshape(mixed.shape[0], mixed.shape[1] * mixed.shape[2])

def reference(tokens, x_weight, dt_weight, bc_weight, conv_x, conv_bc, dt_bias, a_rate, d_skip, norm_gain):
    bc_width = GROUPS * 2 * STATE
    x_pre = jnp.dot(tokens, x_weight, preferred_element_type=jnp.float32).astype(jnp.bfloat16)
    dt_raw = jnp.dot(tokens, dt_weight, preferred_element_type=jnp.float32)
    bc_cols = jnp.transpose(bc_weight, (1, 0, 2)).reshape(D, bc_width)
    bc_pre = jnp.dot(tokens, bc_cols, preferred_element_type=jnp.float32).astype(jnp.bfloat16)
    bc_taps = jnp.transpose(conv_bc, (1, 0, 2)).reshape(CONV, bc_width)
    x_conv = causal_conv(x_pre, conv_x)
    bc_conv = causal_conv(bc_pre, bc_taps)
    step_sizes = jax.nn.softplus(dt_raw + dt_bias)
    blocks = TOKENS // SPAN
    log_sums = jnp.cumsum((-a_rate * step_sizes).reshape(blocks, SPAN, HEADS), axis=1)
    x_blocks = x_conv.reshape(blocks, SPAN, HEADS, HEAD_DIM)
    bc_blocks = bc_conv.reshape(blocks, SPAN, GROUPS, 2, STATE)
    step_blocks = step_sizes.reshape(blocks, SPAN, HEADS)

    def advance(carried, block):
        values, key_query, sums_here, sizes_here = block
        inner_terms, states = span_pieces(values, key_query, sums_here, sizes_here)
        mixed = inner_terms + span_reads(key_query[:, :, 1], sums_here, carried) + d_skip[None, :, None] * values.astype(jnp.float32)
        carried = jnp.exp(sums_here[-1])[:, None, None] * carried + states
        return (carried, mixed)
    initial = jnp.zeros((HEADS, HEAD_DIM, STATE), jnp.float32)
    _, mixed = lax.scan(advance, initial, (x_blocks, bc_blocks, log_sums, step_blocks))
    return finish(mixed.reshape(TOKENS, HEADS, HEAD_DIM), norm_gain)
```

```python
import functools

import jax
import jax.numpy as jnp
from jax import lax
from jax.experimental import pallas as pl
from jax.experimental.pallas import tpu as pltpu
from jax.sharding import PartitionSpec as P

MESH = pl.DeviceIdType.MESH

HEADS = 128
HEAD_DIM = 64
STATE = 128
GROUPS = 8
SPAN = 256
CONV = 4


def place():
    c = lax.axis_index("context")
    t = lax.axis_index("tensor")
    return t // 4, c // 8, t % 4, (c // 2) % 4, c % 2


def device(x, y, z_hi, z_lo, core):
    return ((y % 4) * 8 + (z_lo % 4) * 2 + core, (x % 4) * 4 + z_hi % 4)


def along_z(z, by):
    other = (z + by + 16) % 16
    return other // 4, other % 4


def project_kernel(
    tok_ref, w_ref, dt_ref, bc_ref,
    x_out, bc_out, dt_out,
    tok, wb, dts,
    local_sem, tz_s, tz_r, tx_s, tx_r, wz_s, wz_r, bz_s, bz_r,
    wy_s, wy_r, wc_s, wc_r, dz_s, dz_r, dy_s, dy_r, dc_s, dc_r,
):
    x, y, z_hi, z_lo, core = place()
    z = z_hi * 4 + z_lo
    t_own = x * 4 + z_hi
    sibling = device(x, y, z_hi, z_lo, 1 - core)

    def send(src, dst, ssem, rsem, dev):
        copy = pltpu.make_async_remote_copy(
            src_ref=src, dst_ref=dst, send_sem=ssem, recv_sem=rsem, device_id=dev, device_id_type=MESH
        )
        copy.start()
        return copy

    def piece(y_at, z_at, core_at):
        return (y_at % 4) * 8 + (z_at % 4) * 2 + core_at

    own = piece(y, z_lo, core)
    group = x * 2 + z_hi // 2
    local = [
        pltpu.make_async_copy(tok_ref, tok.at[t_own], local_sem.at[0]),
        pltpu.make_async_copy(w_ref, wb.at[own, :, pl.ds(0, 512)], local_sem.at[1]),
        pltpu.make_async_copy(bc_ref.at[group], wb.at[own, :, pl.ds(512, 256)], local_sem.at[2]),
    ]
    for copy in local:
        copy.start()
    square = jnp.concatenate([dt_ref[...].astype(jnp.float32), jnp.zeros((128, 120), jnp.float32)], 1)
    dts[core, y, z_lo] = square.T[:16].astype(jnp.bfloat16)

    barrier = pltpu.get_barrier_semaphore()
    partners = [device(x, y, z_hi + 1, z_lo, core), device(x, y, z_hi + 3, z_lo, core), sibling]
    for by in (1, 2, 3):
        partners.append(device(x + by, y, z_hi, z_lo, core))
        partners.append(device(x, y + by, z_hi, z_lo, core))
        partners.append(device(x, y, z_hi, z_lo + by, core))
    for by in (1, -1, 2, -2):
        partners.append(device(x, y, *along_z(z, by), core))
    for partner in partners:
        pl.semaphore_signal(barrier, inc=1, device_id=partner, device_id_type=MESH)
    pl.semaphore_wait(barrier, len(partners))

    started = []
    dz = [
        send(dts.at[core, y, z_lo], dts.at[core, y, z_lo], dz_s.at[by], dz_r.at[by], device(x, y, z_hi, z_lo + by, core))
        for by in (1, 2, 3)
    ]
    wz = [
        send(w_ref, wb.at[own, :, pl.ds(0, 512)], wz_s.at[by], wz_r.at[by], device(x, y, z_hi, z_lo + by, core))
        for by in (1, 2, 3)
    ]
    bz = []
    for i, (by, first, count) in enumerate(((1, 0, 128), (-1, 0, 128), (2, 0, 64), (-2, 64, 64))):
        hi, lo = along_z(z, by)
        bz.append(
            send(
                bc_ref.at[x * 2 + hi // 2, pl.ds(first, count)],
                wb.at[own, pl.ds(first, count), pl.ds(512, 256)],
                bz_s.at[i], bz_r.at[i], device(x, y, hi, lo, core),
            )
        )
    tz = [
        send(tok_ref, tok.at[t_own], tz_s.at[0], tz_r.at[0], device(x, y, z_hi + 1, z_lo, core)),
        send(tok_ref, tok.at[t_own], tz_s.at[1], tz_r.at[1], device(x, y, z_hi + 3, z_lo, core)),
    ]
    for copy in local:
        copy.wait()

    tx = []

    def tokens_along_x(k, hi):
        slot = tok.at[x * 4 + hi]
        for by in (1, 2, 3):
            tx.append(
                send(slot, slot, tx_s.at[k, by], tx_r.at[k, by], device(x + by, y, z_hi, z_lo, core))
            )

    wy = {}

    def rows_along_y(k):
        slot = wb.at[piece(y, z_lo + k, core)]
        wy[k, 0] = send(slot, slot, wy_s.at[k, 0], wy_r.at[k, 0], device(x, y + 1, z_hi, z_lo, core))
        wy[k, 1] = send(slot, slot, wy_s.at[k, 1], wy_r.at[k, 1], device(x, y + 3, z_hi, z_lo, core))

    def relay_along_y(k):
        wy[k, 0].wait_recv()
        half = wb.at[piece(y + 3, z_lo + k, core), pl.ds(0, 64)]
        wy[k, 2] = send(half, half, wy_s.at[k, 2], wy_r.at[k, 2], device(x, y + 1, z_hi, z_lo, core))
        wy[k, 1].wait_recv()
        half = wb.at[piece(y + 1, z_lo + k, core), pl.ds(64, 64)]
        wy[k, 3] = send(half, half, wy_s.at[k, 3], wy_r.at[k, 3], device(x, y + 3, z_hi, z_lo, core))
        to_sibling(k, 3)
        to_sibling(k, 1)

    wc = []

    def to_sibling(k, by):
        slot = wb.at[piece(y + by, z_lo + k, core)]
        wc.append(send(slot, slot, wc_s.at[k, by], wc_r.at[k, by], sibling))

    rows_along_y(0)
    tokens_along_x(0, z_hi)
    to_sibling(0, 0)

    for copy in dz:
        copy.wait_recv()
    block = dts.at[core, y]
    dy = [
        send(block, block, dy_s.at[by], dy_r.at[by], device(x, y + by, z_hi, z_lo, core)) for by in (1, 2, 3)
    ]

    for copy in bz:
        copy.wait_recv()
    for by in (1, 3, 2):
        wz[by - 1].wait_recv()
        rows_along_y(4 - by)
        to_sibling(4 - by, 0)
    relay_along_y(0)
    for copy in dy:
        copy.wait_recv()
    block = dts.at[core]
    dc = send(block, block, dc_s, dc_r, sibling)

    tz[0].wait_recv()
    half = tok.at[x * 4 + (z_hi + 3) % 4, :, pl.ds(0, 2048)]
    tz.append(send(half, half, tz_s.at[2], tz_r.at[2], device(x, y, z_hi + 1, z_lo, core)))
    tz[1].wait_recv()
    half = tok.at[x * 4 + (z_hi + 1) % 4, :, pl.ds(2048, 2048)]
    tz.append(send(half, half, tz_s.at[3], tz_r.at[3], device(x, y, z_hi + 3, z_lo, core)))
    tokens_along_x(1, (z_hi + 3) % 4)
    tokens_along_x(2, (z_hi + 1) % 4)

    for k in (3, 1, 2):
        relay_along_y(k)
    tz[2].wait_recv()
    tz[3].wait_recv()
    tokens_along_x(3, (z_hi + 2) % 4)
    for k in (0, 3, 1, 2):
        wy[k, 2].wait_recv()
        wy[k, 3].wait_recv()
        to_sibling(k, 2)
    for copy in tx:
        copy.wait_recv()
    dc.wait_recv()
    for copy in wc:
        copy.wait_recv()

    rows = tok[...].reshape(256, 4096)
    dt_cols = jnp.concatenate([dts[p % 2, p // 8, (p // 2) % 4] for p in range(32)], 1)
    dt_out[...] = lax.dot_general(rows, dt_cols, (((1,), (1,)), ((), ())), preferred_element_type=jnp.float32)
    both = jnp.dot(rows, wb[...].reshape(4096, 768), preferred_element_type=jnp.float32)
    x_out[...] = both[:, :512].astype(jnp.bfloat16)
    bc_out[...] = both[:, 512:].astype(jnp.bfloat16)

    for copy in dz + wz + bz + tz + tx + list(wy.values()) + wc + dy + [dc]:
        copy.wait_send()


def project(tokens, x_weight, dt_weight, bc_weight):
    dma = pltpu.SemaphoreType.DMA
    return pl.pallas_call(
        project_kernel,
        out_shape=(
            jax.ShapeDtypeStruct((256, 512), jnp.bfloat16),
            jax.ShapeDtypeStruct((256, 256), jnp.bfloat16),
            jax.ShapeDtypeStruct((256, 16), jnp.float32),
        ),
        in_specs=[
            pl.BlockSpec(memory_space=pl.ANY),
            pl.BlockSpec(memory_space=pl.ANY),
            pl.BlockSpec(memory_space=pltpu.VMEM),
            pl.BlockSpec(memory_space=pl.ANY),
        ],
        out_specs=[pl.BlockSpec(memory_space=pltpu.VMEM)] * 3,
        scratch_shapes=[
            pltpu.VMEM((16, 16, 4096), jnp.bfloat16),
            pltpu.VMEM((32, 128, 768), jnp.bfloat16),
            pltpu.VMEM((2, 4, 4, 16, 128), jnp.bfloat16),
            dma((3,)),
            dma((4,)), dma((4,)), dma((4, 4)), dma((4, 4)), dma((4,)), dma((4,)), dma((4,)), dma((4,)),
            dma((4, 4)), dma((4, 4)), dma((4, 4)), dma((4, 4)), dma((4,)), dma((4,)), dma((4,)), dma((4,)), dma, dma,
        ],
        compiler_params=pltpu.CompilerParams(collective_id=0, has_side_effects=True, vmem_limit_bytes=50 * 2**20),
        name="project",
    )(tokens, x_weight, dt_weight, bc_weight)


def shifted(block, axis, distance):
    devices = range(lax.axis_size(axis))
    route = [(i - distance, i) for i in devices if i - distance in devices]
    return lax.ppermute(block, axis, route)


def carried_in(part, axis, combine, identity):
    place = lax.axis_index(axis)
    gathered = jax.tree.map(lambda a: lax.all_gather(a, axis), part)
    state = jax.tree.map(lambda a, e: jnp.zeros_like(a) + jnp.asarray(e, a.dtype), part, identity)

    def one(hop, state):
        return combine(
            state, jax.tree.map(lambda a: lax.dynamic_index_in_dim(a, hop, 0, False), gathered)
        )

    return lax.fori_loop(0, place, one, state)


def causal_conv(previous, values, taps):
    count = values.shape[0]
    joined = jnp.concatenate([previous, values], 0).astype(jnp.float32)
    total = jnp.zeros(values.shape, jnp.float32)
    for offset in range(CONV):
        total = total + taps[offset].astype(jnp.float32) * joined[offset : offset + count]
    return jax.nn.silu(total).astype(jnp.bfloat16)


def span_pieces(values, key_query, log_sums, step_sizes):
    length, heads_n, head_width = values.shape
    groups_n = key_query.shape[1]
    per_group = heads_n // groups_n
    inputs_b = key_query[:, :, 0]
    outputs_c = key_query[:, :, 1]
    scores = jnp.einsum("tgn,sgn->gts", outputs_c, inputs_b, preferred_element_type=jnp.float32)
    positions = jnp.arange(length)
    causal_mask = positions[:, None] >= positions[None, :]
    log_gaps = log_sums.T[:, :, None] - log_sums.T[:, None, :]
    decay_table = jnp.where(causal_mask, jnp.exp(jnp.where(causal_mask, log_gaps, 0.0)), 0.0)
    mixing = (
        scores[:, None]
        * decay_table.reshape(groups_n, per_group, length, length)
        * step_sizes.T.reshape(groups_n, per_group, 1, length)
    ).astype(jnp.bfloat16)
    grouped = values.reshape(length, groups_n, per_group, head_width)
    inner_terms = jnp.einsum(
        "gjts,sgjp->tgjp", mixing, grouped, preferred_element_type=jnp.float32
    ).reshape(length, heads_n, head_width)
    tail_weight = jnp.exp(log_sums[-1][None, :] - log_sums) * step_sizes
    weighted = values.astype(jnp.float32) * tail_weight[:, :, None]
    states = jnp.einsum(
        "sgjp,sgn->gjpn",
        weighted.reshape(length, groups_n, per_group, head_width),
        inputs_b.astype(jnp.float32),
        precision=lax.Precision.HIGHEST,
    ).reshape(heads_n, head_width, inputs_b.shape[2])
    return (inner_terms, states)


def span_reads(outputs_c, log_sums, start_state):
    length, groups_n, state_width = outputs_c.shape
    heads_n, head_width = (start_state.shape[0], start_state.shape[1])
    per_group = heads_n // groups_n
    reads = jnp.einsum(
        "tgn,gjpn->tgjp",
        outputs_c.astype(jnp.float32),
        start_state.reshape(groups_n, per_group, head_width, state_width),
        precision=lax.Precision.HIGHEST,
    )
    return reads.reshape(length, heads_n, head_width) * jnp.exp(log_sums)[:, :, None]


def finish(mixed, norm_gain):
    mean_square = jnp.mean(mixed * mixed, axis=-1, keepdims=True)
    normed = (
        mixed * lax.rsqrt(mean_square + 1e-05) * norm_gain.reshape(mixed.shape[1], mixed.shape[2])
    )
    return normed.astype(jnp.bfloat16).reshape(mixed.shape[0], mixed.shape[1] * mixed.shape[2])


def local(
    tokens, x_weight, dt_weight, bc_weight, conv_x, conv_bc, dt_bias, a_rate, d_skip, norm_gain
):
    heads_here = dt_weight.shape[1]
    per_group = HEADS // GROUPS
    groups_here = max(1, heads_here // per_group)
    first_group = lax.axis_index("tensor") * heads_here // per_group
    taps_local = lax.dynamic_slice_in_dim(conv_bc, first_group, groups_here, 0)
    bc_taps = jnp.transpose(taps_local, (1, 0, 2)).reshape(CONV, groups_here * 2 * STATE)
    x_pre, bc_pre, dt_wide = project(tokens, x_weight, dt_weight, bc_weight)
    dt_raw = dt_wide[:, :heads_here]
    rows_here = x_pre.shape[0]
    blocks = rows_here // SPAN
    rim_x, rim_bc = shifted(
        (x_pre[rows_here - CONV + 1 :], bc_pre[rows_here - CONV + 1 :]), "context", 1
    )
    x_conv = causal_conv(rim_x, x_pre, conv_x)
    bc_conv = causal_conv(rim_bc, bc_pre, bc_taps)
    step_sizes = jax.nn.softplus(dt_raw + dt_bias)
    log_sums = jnp.cumsum((-a_rate * step_sizes).reshape(blocks, SPAN, heads_here), axis=1)
    x_blocks = x_conv.reshape(blocks, SPAN, heads_here, HEAD_DIM)
    bc_blocks = bc_conv.reshape(blocks, SPAN, groups_here, 2, STATE)
    step_blocks = step_sizes.reshape(blocks, SPAN, heads_here)
    inner_terms, block_states = jax.vmap(span_pieces)(x_blocks, bc_blocks, log_sums, step_blocks)
    block_logs = log_sums[:, -1, :]
    carried = jnp.zeros((heads_here, HEAD_DIM, STATE), jnp.float32)
    starts = [carried]
    carried = jnp.exp(block_logs[0])[:, None, None] * carried + block_states[0]
    total_log = jnp.sum(block_logs, 0)

    def combine(earlier, later):
        return (earlier[0] + later[0], jnp.exp(later[0])[:, None, None] * earlier[1] + later[1])

    identity = (jnp.zeros((heads_here,), jnp.float32), jnp.zeros_like(carried))
    _, incoming = carried_in((total_log, carried), "context", combine, identity)
    lead_logs = jnp.cumsum(block_logs, 0) - block_logs
    start_states = jnp.stack(starts) + jnp.exp(lead_logs)[:, :, None, None] * incoming[None]
    reads = jax.vmap(span_reads)(bc_blocks[:, :, :, 1], log_sums, start_states)
    mixed = inner_terms + reads + d_skip[None, None, :, None] * x_blocks.astype(jnp.float32)
    return finish(mixed.reshape(rows_here, heads_here, HEAD_DIM), norm_gain)


def solution(mesh):
    in_specs = (
        P(("context", "tensor"), None),
        P("context", "tensor"),
        P("context", "tensor"),
        P(None, "context", None),
        P(None, "tensor"),
        P(),
        P("tensor"),
        P("tensor"),
        P("tensor"),
        P("tensor"),
    )
    out_specs = P("context", "tensor")
    return jax.shard_map(local, mesh=mesh, in_specs=in_specs, out_specs=out_specs, check_vma=False)
```

```python
import jax
import jax.numpy as jnp
from jax import lax
from jax.experimental import pallas as pl
from jax.experimental.pallas import tpu as pltpu
from jax.sharding import PartitionSpec as P

MESH = pl.DeviceIdType.MESH

HEAD_DIM = 64
STATE = 128
SPAN = 256
CONV = 4
CONTEXTS = 32


def place():
    c = lax.axis_index("context")
    t = lax.axis_index("tensor")
    return t // 4, c // 8, t % 4, (c // 2) % 4, c % 2


def device(x, y, z_hi, z_lo, core):
    return ((y % 4) * 8 + (z_lo % 4) * 2 + core, (x % 4) * 4 + z_hi % 4)


def along_z(z, by):
    other = (z + by + 16) % 16
    return other // 4, other % 4


def layer_kernel(
    tok_ref, w_ref, dt_ref, bc_ref, conv_x_ref, conv_bc_ref, bias_ref, rate_ref, skip_ref, gain_ref,
    out_ref,
    tok, wb, dts, pre, inner, decays, mine, theirs, leaving, arriving,
    local_sem, tz_s, tz_r, tx_s, tx_r, wz_s, wz_r, bz_s, bz_r,
    wy_s, wy_r, wc_s, wc_r, dz_s, dz_r, dy_s, dy_r, dc_s, dc_r,
    rim_s, rim_r, decay_s, decay_r, state_s, state_r, start_s, start_r,
):
    x, y, z_hi, z_lo, core = place()
    z = z_hi * 4 + z_lo
    t_own = x * 4 + z_hi
    sibling = device(x, y, z_hi, z_lo, 1 - core)

    def send(src, dst, ssem, rsem, dev):
        copy = pltpu.make_async_remote_copy(
            src_ref=src, dst_ref=dst, send_sem=ssem, recv_sem=rsem, device_id=dev, device_id_type=MESH
        )
        copy.start()
        return copy

    def piece(y_at, z_at, core_at):
        return (y_at % 4) * 8 + (z_at % 4) * 2 + core_at

    own = piece(y, z_lo, core)
    group = x * 2 + z_hi // 2
    local = [
        pltpu.make_async_copy(tok_ref, tok.at[t_own], local_sem.at[0]),
        pltpu.make_async_copy(w_ref, wb.at[own, :, pl.ds(0, 512)], local_sem.at[1]),
        pltpu.make_async_copy(bc_ref.at[group], wb.at[own, :, pl.ds(512, 256)], local_sem.at[2]),
    ]
    for copy in local:
        copy.start()
    square = jnp.concatenate([dt_ref[...].astype(jnp.float32), jnp.zeros((128, 120), jnp.float32)], 1)
    dts[core, y, z_lo] = square.T[:16].astype(jnp.bfloat16)

    barrier = pltpu.get_barrier_semaphore()
    partners = [device(x, y, z_hi + 1, z_lo, core), device(x, y, z_hi + 3, z_lo, core), sibling]
    for by in (1, 2, 3):
        partners.append(device(x + by, y, z_hi, z_lo, core))
        partners.append(device(x, y + by, z_hi, z_lo, core))
        partners.append(device(x, y, z_hi, z_lo + by, core))
    for by in (1, -1, 2, -2):
        partners.append(device(x, y, *along_z(z, by), core))
    c = lax.axis_index("context")
    for by in (1, CONTEXTS - 1):
        partners.append(((c + by) % CONTEXTS, t_own))
    for partner in partners:
        pl.semaphore_signal(barrier, inc=1, device_id=partner, device_id_type=MESH)
    pl.semaphore_wait(barrier, len(partners))

    started = []
    dz = [
        send(dts.at[core, y, z_lo], dts.at[core, y, z_lo], dz_s.at[by], dz_r.at[by], device(x, y, z_hi, z_lo + by, core))
        for by in (1, 2, 3)
    ]
    wz = [
        send(w_ref, wb.at[own, :, pl.ds(0, 512)], wz_s.at[by], wz_r.at[by], device(x, y, z_hi, z_lo + by, core))
        for by in (1, 2, 3)
    ]
    bz = []
    for i, (by, first, count) in enumerate(((1, 0, 128), (-1, 0, 128), (2, 0, 64), (-2, 64, 64))):
        hi, lo = along_z(z, by)
        bz.append(
            send(
                bc_ref.at[x * 2 + hi // 2, pl.ds(first, count)],
                wb.at[own, pl.ds(first, count), pl.ds(512, 256)],
                bz_s.at[i], bz_r.at[i], device(x, y, hi, lo, core),
            )
        )
    tz = [
        send(tok_ref, tok.at[t_own], tz_s.at[0], tz_r.at[0], device(x, y, z_hi + 1, z_lo, core)),
        send(tok_ref, tok.at[t_own], tz_s.at[1], tz_r.at[1], device(x, y, z_hi + 3, z_lo, core)),
    ]
    for copy in local:
        copy.wait()

    tx = []

    def tokens_along_x(k, hi):
        slot = tok.at[x * 4 + hi]
        for by in (1, 2, 3):
            tx.append(
                send(slot, slot, tx_s.at[k, by], tx_r.at[k, by], device(x + by, y, z_hi, z_lo, core))
            )

    wy = {}

    def rows_along_y(k):
        slot = wb.at[piece(y, z_lo + k, core)]
        wy[k, 0] = send(slot, slot, wy_s.at[k, 0], wy_r.at[k, 0], device(x, y + 1, z_hi, z_lo, core))
        wy[k, 1] = send(slot, slot, wy_s.at[k, 1], wy_r.at[k, 1], device(x, y + 3, z_hi, z_lo, core))

    def relay_along_y(k):
        wy[k, 0].wait_recv()
        half = wb.at[piece(y + 3, z_lo + k, core), pl.ds(0, 64)]
        wy[k, 2] = send(half, half, wy_s.at[k, 2], wy_r.at[k, 2], device(x, y + 1, z_hi, z_lo, core))
        wy[k, 1].wait_recv()
        half = wb.at[piece(y + 1, z_lo + k, core), pl.ds(64, 64)]
        wy[k, 3] = send(half, half, wy_s.at[k, 3], wy_r.at[k, 3], device(x, y + 3, z_hi, z_lo, core))
        to_sibling(k, 3)
        to_sibling(k, 1)

    wc = []

    def to_sibling(k, by):
        slot = wb.at[piece(y + by, z_lo + k, core)]
        wc.append(send(slot, slot, wc_s.at[k, by], wc_r.at[k, by], sibling))

    rows_along_y(0)
    tokens_along_x(0, z_hi)
    to_sibling(0, 0)

    for copy in dz:
        copy.wait_recv()
    block = dts.at[core, y]
    dy = [
        send(block, block, dy_s.at[by], dy_r.at[by], device(x, y + by, z_hi, z_lo, core)) for by in (1, 2, 3)
    ]

    for copy in bz:
        copy.wait_recv()
    for by in (1, 3, 2):
        wz[by - 1].wait_recv()
        rows_along_y(4 - by)
        to_sibling(4 - by, 0)
    relay_along_y(0)
    for copy in dy:
        copy.wait_recv()
    block = dts.at[core]
    dc = send(block, block, dc_s, dc_r, sibling)

    tz[0].wait_recv()
    half = tok.at[x * 4 + (z_hi + 3) % 4, :, pl.ds(0, 2048)]
    tz.append(send(half, half, tz_s.at[2], tz_r.at[2], device(x, y, z_hi + 1, z_lo, core)))
    tz[1].wait_recv()
    half = tok.at[x * 4 + (z_hi + 1) % 4, :, pl.ds(2048, 2048)]
    tz.append(send(half, half, tz_s.at[3], tz_r.at[3], device(x, y, z_hi + 3, z_lo, core)))
    tokens_along_x(1, (z_hi + 3) % 4)
    tokens_along_x(2, (z_hi + 1) % 4)

    for k in (3, 1, 2):
        relay_along_y(k)
    tz[2].wait_recv()
    tz[3].wait_recv()
    tokens_along_x(3, (z_hi + 2) % 4)
    for k in (0, 3, 1, 2):
        wy[k, 2].wait_recv()
        wy[k, 3].wait_recv()
        to_sibling(k, 2)
    for copy in tx:
        copy.wait_recv()
    dc.wait_recv()

    c = lax.axis_index("context")
    t = lax.axis_index("tensor")

    def to_all_contexts(source, slots, ssem, rsem):
        def one(step, carry):
            j = (c + step) % CONTEXTS
            send(source(j), slots.at[c], ssem, rsem, (j, t))
            return carry

        lax.fori_loop(1, CONTEXTS, one, 0)

    def all_of(slots, ssem, rsem):
        several = slots.at[pl.ds(0, CONTEXTS - 1)]
        return pltpu.make_async_remote_copy(
            src_ref=several, dst_ref=several, send_sem=ssem, recv_sem=rsem, device_id=sibling, device_id_type=MESH
        )

    rows = tok[...].reshape(SPAN, 4096)
    dt_cols = jnp.concatenate([dts[p % 2, p // 8, (p // 2) % 4] for p in range(32)], 1)
    dt_raw = lax.dot_general(rows, dt_cols, (((1,), (1,)), ((), ())), preferred_element_type=jnp.float32)
    raw = jnp.concatenate([dt_raw, jnp.zeros((SPAN, 112), jnp.float32)], 1).T[:8]
    head_row = lax.broadcasted_iota(jnp.int32, (8, SPAN), 0)

    def per_head(ref):
        return sum(jnp.where(head_row == h, ref[h], 0.0) for h in range(8))

    raw = raw + per_head(bias_ref)
    steps = jnp.maximum(raw, 0.0) + jnp.log1p(jnp.exp(-jnp.abs(raw)))
    upto = lax.broadcasted_iota(jnp.int32, (SPAN, SPAN), 0) <= lax.broadcasted_iota(jnp.int32, (SPAN, SPAN), 1)
    sums = jnp.dot(
        -per_head(rate_ref) * steps, upto.astype(jnp.float32),
        precision=lax.Precision.HIGHEST, preferred_element_type=jnp.float32,
    )
    last = jnp.broadcast_to(sums[:, SPAN - 1 :], (8, SPAN))
    tails = jnp.exp(last - sums) * steps
    columns = jnp.concatenate([sums, tails, jnp.zeros((112, SPAN), jnp.float32)], 0).T
    low_lanes = lax.broadcasted_iota(jnp.int32, (1, 128), 1) < HEAD_DIM
    whole = jnp.exp(last[:, :128])
    decays[c] = jnp.concatenate(
        [jnp.where(low_lanes, whole[2 * b : 2 * b + 1], whole[2 * b + 1 : 2 * b + 2]) for b in range(4)]
        + [jnp.zeros((4, 128), jnp.float32)],
        0,
    )
    to_all_contexts(lambda j: decays.at[c], decays, decay_s, decay_r)

    def spread(first):
        return jnp.concatenate(
            [
                jnp.where(low_lanes, columns[:, first + 2 * b : first + 2 * b + 1], columns[:, first + 2 * b + 1 : first + 2 * b + 2])
                for b in range(4)
            ],
            1,
        )

    for copy in wc:
        copy.wait_recv()
    both = jnp.dot(rows, wb[...].reshape(4096, 768), preferred_element_type=jnp.float32)
    pre[8:] = both.astype(jnp.bfloat16).astype(jnp.float32)
    rim = send(
        pre.at[pl.ds(SPAN, 8)], pre.at[pl.ds(0, 8)], rim_s, rim_r, ((c + 1) % CONTEXTS, t)
    )
    rim.wait_recv()

    @pl.when(c == 0)
    def _():
        pre[:8] = jnp.zeros((8, 768), jnp.float32)

    def convolved(first, width, taps):
        total = sum(
            taps[k : k + 1].astype(jnp.float32) * pre[5 + k : 5 + k + SPAN, first : first + width] for k in range(CONV)
        )
        return (total / (1.0 + jnp.exp(-total))).astype(jnp.bfloat16)

    b_conv = convolved(512, STATE, conv_bc_ref[group][:, :STATE])
    c_conv = convolved(640, STATE, conv_bc_ref[group][:, STATE:])
    x_conv = convolved(0, 512, conv_x_ref[...])

    weighted = (x_conv.astype(jnp.float32) * spread(8)).astype(jnp.bfloat16)
    state = lax.dot_general(b_conv, weighted, (((0,), (0,)), ((), ())), preferred_element_type=jnp.float32)
    state = state.astype(jnp.bfloat16)
    for j in range(CONTEXTS):
        mine[j] = state[16 * (j // 4) : 16 * (j // 4 + 1), 128 * (j % 4) : 128 * (j % 4 + 1)]
    to_all_contexts(lambda j: mine.at[j], theirs, state_s, state_r)
    theirs[c] = mine[c]

    scores = lax.dot_general(c_conv, b_conv, (((1,), (1,)), ((), ())), preferred_element_type=jnp.float32)
    upto = lax.broadcasted_iota(jnp.int32, (SPAN, SPAN), 0) >= lax.broadcasted_iota(jnp.int32, (SPAN, SPAN), 1)
    scores = jnp.where(upto, scores, 0.0)

    def within(h):
        gaps = jnp.minimum(columns[:, h : h + 1] - sums[h : h + 1], 0.0)
        mixing = (scores * jnp.exp(gaps) * steps[h : h + 1]).astype(jnp.bfloat16)
        here = x_conv[:, h * HEAD_DIM : (h + 1) * HEAD_DIM]
        return (
            jnp.dot(mixing, here, preferred_element_type=jnp.float32) + skip_ref[h] * here.astype(jnp.float32)
        )

    for b in range(4):
        inner[:, 128 * b : 128 * (b + 1)] = jnp.concatenate([within(2 * b), within(2 * b + 1)], 1)

    all_of(decays, decay_s, decay_r).wait_recv()
    all_of(theirs, state_s, state_r).wait_recv()
    carried = jnp.zeros((16, 128), jnp.float32)
    for j in range(CONTEXTS):
        leaving[j] = carried.astype(jnp.bfloat16)
        carried = decays[j, pl.ds(c % 4, 1)] * carried + theirs[j].astype(jnp.float32)
    to_all_contexts(lambda j: leaving.at[j], arriving, start_s, start_r)
    arriving[c] = leaving[c]
    growth = jnp.exp(spread(0))
    all_of(arriving, start_s, start_r).wait_recv()
    start = jnp.concatenate(
        [jnp.concatenate([arriving[4 * i + b] for b in range(4)], 1) for i in range(8)], 0
    )
    mixed = inner[...] + growth * jnp.dot(c_conv, start, preferred_element_type=jnp.float32)
    same_head = (
        lax.broadcasted_iota(jnp.int32, (128, 128), 0) // HEAD_DIM == lax.broadcasted_iota(jnp.int32, (128, 128), 1) // HEAD_DIM
    ).astype(jnp.bfloat16)
    for b in range(4):
        part = mixed[:, 128 * b : 128 * (b + 1)]
        square = part * part
        upper = square.astype(jnp.bfloat16)
        lower = (square - upper.astype(jnp.float32)).astype(jnp.bfloat16)
        total = jnp.dot(upper, same_head, preferred_element_type=jnp.float32) + jnp.dot(
            lower, same_head, preferred_element_type=jnp.float32
        )
        scaled = part * lax.rsqrt(total * (1.0 / HEAD_DIM) + 1e-05) * gain_ref[:, 128 * b : 128 * (b + 1)]
        out_ref[:, 128 * b : 128 * (b + 1)] = scaled.astype(jnp.bfloat16)

    for copy in dz + wz + bz + tz + tx + list(wy.values()) + wc + dy + [dc, rim]:
        copy.wait_send()
    all_of(decays, decay_s, decay_r).wait_send()
    all_of(mine, state_s, state_r).wait_send()
    all_of(leaving, start_s, start_r).wait_send()


def local(
    tokens, x_weight, dt_weight, bc_weight, conv_x, conv_bc, dt_bias, a_rate, d_skip, norm_gain
):
    dma = pltpu.SemaphoreType.DMA
    in_vmem = pl.BlockSpec(memory_space=pltpu.VMEM)
    in_smem = pl.BlockSpec(memory_space=pltpu.SMEM)
    anywhere = pl.BlockSpec(memory_space=pl.ANY)
    return pl.pallas_call(
        layer_kernel,
        out_shape=jax.ShapeDtypeStruct((SPAN, 512), jnp.bfloat16),
        in_specs=[anywhere, anywhere, in_vmem, anywhere, in_vmem, in_vmem, in_smem, in_smem, in_smem, in_vmem],
        out_specs=in_vmem,
        scratch_shapes=[
            pltpu.VMEM((16, 16, 4096), jnp.bfloat16),
            pltpu.VMEM((32, 128, 768), jnp.bfloat16),
            pltpu.VMEM((2, 4, 4, 16, 128), jnp.bfloat16),
            pltpu.VMEM((8 + SPAN, 768), jnp.float32),
            pltpu.VMEM((SPAN, 512), jnp.float32),
            pltpu.VMEM((CONTEXTS, 8, 128), jnp.float32),
            pltpu.VMEM((CONTEXTS, 16, 128), jnp.bfloat16),
            pltpu.VMEM((CONTEXTS, 16, 128), jnp.bfloat16),
            pltpu.VMEM((CONTEXTS, 16, 128), jnp.bfloat16),
            pltpu.VMEM((CONTEXTS, 16, 128), jnp.bfloat16),
            dma((3,)),
            dma((4,)), dma((4,)), dma((4, 4)), dma((4, 4)), dma((4,)), dma((4,)), dma((4,)), dma((4,)),
            dma((4, 4)), dma((4, 4)), dma((4, 4)), dma((4, 4)), dma((4,)), dma((4,)), dma((4,)), dma((4,)), dma, dma,
            dma, dma, dma, dma, dma, dma, dma, dma,
        ],
        compiler_params=pltpu.CompilerParams(collective_id=0, has_side_effects=True, vmem_limit_bytes=50 * 2**20),
        name="layer",
    )(tokens, x_weight, dt_weight, bc_weight, conv_x, conv_bc, dt_bias, a_rate, d_skip, norm_gain.reshape(1, 512))


def solution(mesh):
    in_specs = (
        P(("context", "tensor"), None),
        P("context", "tensor"),
        P("context", "tensor"),
        P(None, "context", None),
        P(None, "tensor"),
        P(),
        P("tensor"),
        P("tensor"),
        P("tensor"),
        P("tensor"),
    )
    out_specs = P("context", "tensor")
    return jax.shard_map(local, mesh=mesh, in_specs=in_specs, out_specs=out_specs, check_vma=False)
```

```python
import jax
import jax.numpy as jnp
from jax import lax
from jax.experimental import pallas as pl
from jax.experimental.pallas import tpu as pltpu
from jax.sharding import PartitionSpec as P

MESH = pl.DeviceIdType.MESH

HEAD_DIM = 64
STATE = 128
SPAN = 256
CONV = 4
CONTEXTS = 32


def place():
    c = lax.axis_index("context")
    t = lax.axis_index("tensor")
    return t // 4, c // 8, t % 4, (c // 2) % 4, c % 2


def device(x, y, z_hi, z_lo, core):
    return ((y % 4) * 8 + (z_lo % 4) * 2 + core, (x % 4) * 4 + z_hi % 4)


def along_z(z, by):
    other = (z + by + 16) % 16
    return other // 4, other % 4


ORDER = ((0, 1, 2, 3), (1, 0, 2, 3), (2, 1, 3, 0), (3, 2, 1, 0))
ONWARD = (None, (1, 1), (-1, -1), (-1, 1))


def pick(index, values):
    out = values[-1]
    for k in range(len(values) - 2, -1, -1):
        out = jnp.where(index == k, values[k], out)
    return out


def layer_kernel(
    tok_ref, w_ref, dt_ref, bc_ref, conv_x_ref, conv_bc_ref, bias_ref, rate_ref, skip_ref, gain_ref,
    out_ref,
    tok, wb, dts, pre, inner, decays, mine, theirs, leaving, arriving,
    local_sem, tz_s, tz_r, tx_s, tx_r, wz_s, wz_r, bz_s, bz_r,
    wy_s, wy_r, wc_s, wc_r, dz_s, dz_r, dy_s, dy_r, dc_s, dc_r,
    rim_s, rim_r, decay_s, decay_r, state_s, state_r, start_s, start_r,
):
    x, y, z_hi, z_lo, core = place()
    z = z_hi * 4 + z_lo
    t_own = x * 4 + z_hi
    c = lax.axis_index("context")
    t = lax.axis_index("tensor")
    sibling = device(x, y, z_hi, z_lo, 1 - core)

    def describe(src, dst, ssem, rsem, dev):
        return pltpu.make_async_remote_copy(
            src_ref=src, dst_ref=dst, send_sem=ssem, recv_sem=rsem, device_id=dev, device_id_type=MESH
        )

    def send(*args):
        copy = describe(*args)
        copy.start()
        return copy

    def piece(y_at, z_at, core_at):
        return (y_at % 4) * 8 + (z_at % 4) * 2 + core_at

    def x_part(ref, p):
        return ref.at[p, :, pl.ds(0, 512)]

    own = piece(y, z_lo, core)
    group = x * 2 + z_hi // 2
    local = [
        pltpu.make_async_copy(w_ref, x_part(wb, own), local_sem.at[1]),
        pltpu.make_async_copy(bc_ref.at[group], wb.at[own, :, pl.ds(512, 256)], local_sem.at[2]),
        pltpu.make_async_copy(tok_ref, tok.at[t_own], local_sem.at[0]),
    ]
    for copy in local:
        copy.start()
    dts[core, y, z_lo] = jnp.concatenate(
        [dt_ref[...].astype(jnp.float32), jnp.zeros((8, 128), jnp.float32)], 0
    ).astype(jnp.bfloat16)

    barrier = pltpu.get_barrier_semaphore()
    partners = [device(x, y, z_hi + 1, z_lo, core), device(x, y, z_hi + 3, z_lo, core), sibling]
    for by in (1, 2, 3):
        partners.append(device(x + by, y, z_hi, z_lo, core))
        partners.append(device(x, y + by, z_hi, z_lo, core))
        partners.append(device(x, y, z_hi, z_lo + by, core))
    for by in (1, -1, 2, -2):
        partners.append(device(x, y, *along_z(z, by), core))
    for by in (1, CONTEXTS - 1):
        partners.append(((c + by) % CONTEXTS, t))
    for partner in partners:
        pl.semaphore_signal(barrier, inc=1, device_id=partner, device_id_type=MESH)
    pl.semaphore_wait(barrier, len(partners))

    arrival = [pick(z_lo, [row[j] for row in ORDER]) for j in range(4)]
    guarded = []

    def rows_along_z(z_at, onward, sem, condition):
        to = (z_lo + onward + 4) % 4
        number = pick(to, [pick(z_at, [row.index(k) for k in range(4)]) for row in ORDER])
        block = x_part(wb, piece(y, z_at, core))
        copy = describe(block, block, wz_s.at[sem], wz_r.at[number], device(x, y, z_hi, to, core))

        @pl.when(condition)
        def _():
            copy.start()

        guarded.append((condition, copy))

    for copy in local[:2]:
        copy.wait()
    rows_along_z(z_lo, 1, 0, z_lo < 3)
    rows_along_z(z_lo, -1, 1, z_lo > 0)
    bz = []
    for i, (by, first, count) in enumerate(((1, 0, 128), (-1, 0, 128), (2, 0, 64), (-2, 64, 64))):
        hi, lo = along_z(z, by)
        bz.append(
            send(
                bc_ref.at[x * 2 + hi // 2, pl.ds(first, count)],
                wb.at[own, pl.ds(first, count), pl.ds(512, 256)],
                bz_s.at[i], bz_r.at[i], device(x, y, hi, lo, core),
            )
        )
    block = dts.at[core, y, z_lo]
    dz = [send(block, block, dz_s.at[by], dz_r.at[by], device(x, y, z_hi, z_lo + by, core)) for by in (1, 2, 3)]

    wy = {}
    wc = {}

    def to_sibling(j, by):
        slot = wb.at[piece(y + by, arrival[j], core)]
        wc[j, by] = send(slot, slot, wc_s.at[j, by], wc_r.at[j, by], sibling)

    def rows_along_y(j):
        slot = wb.at[piece(y, arrival[j], core)]
        wy[j, 0] = send(slot, slot, wy_s.at[j, 0], wy_r.at[j, 0], device(x, y + 1, z_hi, z_lo, core))
        wy[j, 1] = send(slot, slot, wy_s.at[j, 1], wy_r.at[j, 1], device(x, y + 3, z_hi, z_lo, core))
        to_sibling(j, 0)

    def next_rows(j):
        block = x_part(wb, piece(y, arrival[j], core))
        describe(block, block, wz_s.at[0], wz_r.at[j], sibling).wait_recv()
        rows_along_z(arrival[j], jnp.where(z_lo == 1, *ONWARD[j]), 1 + j, (z_lo == 1) | (z_lo == 2))
        rows_along_y(j)

    def relay_along_y(j):
        wy[j, 0].wait_recv()
        half = wb.at[piece(y + 3, arrival[j], core), pl.ds(0, 64)]
        wy[j, 2] = send(half, half, wy_s.at[j, 2], wy_r.at[j, 2], device(x, y + 1, z_hi, z_lo, core))
        wy[j, 1].wait_recv()
        half = wb.at[piece(y + 1, arrival[j], core), pl.ds(64, 64)]
        wy[j, 3] = send(half, half, wy_s.at[j, 3], wy_r.at[j, 3], device(x, y + 3, z_hi, z_lo, core))
        to_sibling(j, 3)
        to_sibling(j, 1)

    def last_along_y(j):
        wy[j, 2].wait_recv()
        wy[j, 3].wait_recv()
        to_sibling(j, 2)

    tx = []
    tz = {}

    def tokens_along_x(k, hi, columns):
        slot = tok.at[x * 4 + hi % 4, :, columns]
        for by in (1, 3, 2):
            i = len(tx)
            tx.append(send(slot, slot, tx_s.at[i], tx_r.at[i], device(x + by, y, z_hi, z_lo, core)))

    halves = (pl.ds(0, 2048), pl.ds(2048, 2048))
    up, down = device(x, y, z_hi + 1, z_lo, core), device(x, y, z_hi + 3, z_lo, core)

    def tokens_along_z():
        for half in range(2):
            block = tok.at[t_own, :, halves[half]]
            tz[0, half] = send(block, block, tz_s.at[0, half], tz_r.at[0, half], up)
            tz[1, half] = send(block, block, tz_s.at[1, half], tz_r.at[1, half], down)

    def relay_tokens(half):
        tz[0, half].wait_recv()
        block = tok.at[x * 4 + (z_hi + 3) % 4, :, pl.ds(half * 2048, 1024)]
        tz[2, half] = send(block, block, tz_s.at[2, half], tz_r.at[2, half], up)
        tz[1, half].wait_recv()
        block = tok.at[x * 4 + (z_hi + 1) % 4, :, pl.ds(half * 2048 + 1024, 1024)]
        tz[3, half] = send(block, block, tz_s.at[3, half], tz_r.at[3, half], down)
        tokens_along_x(1, z_hi + 3, halves[half])
        tokens_along_x(2, z_hi + 1, halves[half])

    def last_tokens(half):
        tz[2, half].wait_recv()
        tz[3, half].wait_recv()
        tokens_along_x(3, z_hi + 2, halves[half])

    rows_along_y(0)
    local[2].wait()
    tokens_along_x(0, z_hi, pl.ds(0, 4096))
    for copy in dz:
        copy.wait_recv()
    block = dts.at[core, y]
    dy = [
        send(block, block, dy_s.at[by], dy_r.at[by], device(x, y + by, z_hi, z_lo, core)) for by in (1, 2, 3)
    ]
    for copy in bz:
        copy.wait_recv()
    next_rows(1)
    tokens_along_z()
    next_rows(2)
    relay_tokens(0)
    relay_along_y(0)
    for copy in dy:
        copy.wait_recv()
    block = dts.at[core]
    dc = send(block, block, dc_s, dc_r, sibling)
    next_rows(3)
    relay_tokens(1)
    relay_along_y(1)
    last_tokens(0)
    relay_along_y(2)
    relay_along_y(3)
    last_tokens(1)
    for j in range(4):
        last_along_y(j)
    for copy in tx:
        copy.wait_recv()
    dc.wait_recv()

    def to_all_contexts(source, slots, ssem, rsem):
        def one(step, carry):
            j = (c + step) % CONTEXTS
            send(source(j), slots.at[c], ssem, rsem, (j, t))
            return carry

        lax.fori_loop(1, CONTEXTS, one, 0)

    def all_of(slots, ssem, rsem):
        several = slots.at[pl.ds(0, CONTEXTS - 1)]
        return describe(several, several, ssem, rsem, sibling)

    rows = tok[...].reshape(SPAN, 4096)
    dt_cols = jnp.concatenate([dts[p % 2, p // 8, (p // 2) % 4] for p in range(32)], 1)
    dt_raw = lax.dot_general(rows, dt_cols, (((1,), (1,)), ((), ())), preferred_element_type=jnp.float32)
    raw = jnp.concatenate([dt_raw, jnp.zeros((SPAN, 112), jnp.float32)], 1).T[:8]
    head_row = lax.broadcasted_iota(jnp.int32, (8, SPAN), 0)

    def per_head(ref):
        return sum(jnp.where(head_row == h, ref[h], 0.0) for h in range(8))

    raw = raw + per_head(bias_ref)
    steps = jnp.maximum(raw, 0.0) + jnp.log1p(jnp.exp(-jnp.abs(raw)))
    upto = lax.broadcasted_iota(jnp.int32, (SPAN, SPAN), 0) <= lax.broadcasted_iota(jnp.int32, (SPAN, SPAN), 1)
    sums = jnp.dot(
        -per_head(rate_ref) * steps, upto.astype(jnp.float32),
        precision=lax.Precision.HIGHEST, preferred_element_type=jnp.float32,
    )
    last = jnp.broadcast_to(sums[:, SPAN - 1 :], (8, SPAN))
    tails = jnp.exp(last - sums) * steps
    columns = jnp.concatenate([sums, tails, jnp.zeros((112, SPAN), jnp.float32)], 0).T
    low_lanes = lax.broadcasted_iota(jnp.int32, (1, 128), 1) < HEAD_DIM
    whole = jnp.exp(last[:, :128])
    decays[c] = jnp.concatenate(
        [jnp.where(low_lanes, whole[2 * b : 2 * b + 1], whole[2 * b + 1 : 2 * b + 2]) for b in range(4)]
        + [jnp.zeros((4, 128), jnp.float32)],
        0,
    )
    to_all_contexts(lambda j: decays.at[c], decays, decay_s, decay_r)

    def spread(first):
        return jnp.concatenate(
            [
                jnp.where(low_lanes, columns[:, first + 2 * b : first + 2 * b + 1], columns[:, first + 2 * b + 1 : first + 2 * b + 2])
                for b in range(4)
            ],
            1,
        )

    both = jnp.zeros((SPAN, 768), jnp.float32)
    for by in (0, 1, 3, 2):
        for j in range(4):
            wc[j, by].wait_recv()
        at = (y + by) % 4
        some = tok[:, :, pl.ds(pl.multiple_of(at * 1024, 1024), 1024)].reshape(SPAN, 1024)
        both += jnp.dot(some, wb[pl.ds(at * 8, 8)].reshape(1024, 768), preferred_element_type=jnp.float32)
    pre[8:] = both.astype(jnp.bfloat16).astype(jnp.float32)
    rim = send(
        pre.at[pl.ds(SPAN, 8)], pre.at[pl.ds(0, 8)], rim_s, rim_r, ((c + 1) % CONTEXTS, t)
    )
    x_taps = conv_x_ref[...].astype(jnp.float32)
    bc_taps = conv_bc_ref[group].astype(jnp.float32)

    def convolved(first, width, taps, start, count):
        total = sum(
            taps[k : k + 1] * pre[start + 5 + k : start + 5 + k + count, first : first + width] for k in range(CONV)
        )
        return total / (1.0 + jnp.exp(-total))

    later = (
        convolved(0, 512, x_taps, 8, SPAN - 8),
        convolved(512, 256, bc_taps, 8, SPAN - 8),
    )
    rim.wait_recv()

    @pl.when(c == 0)
    def _():
        pre[:8] = jnp.zeros((8, 768), jnp.float32)

    earlier = (convolved(0, 512, x_taps, 0, 8), convolved(512, 256, bc_taps, 0, 8))
    x_conv, bc_conv = (
        jnp.concatenate(pair, 0).astype(jnp.bfloat16) for pair in zip(earlier, later)
    )
    b_conv, c_conv = bc_conv[:, :STATE], bc_conv[:, STATE:]

    weighted = (x_conv.astype(jnp.float32) * spread(8)).astype(jnp.bfloat16)
    state = lax.dot_general(b_conv, weighted, (((0,), (0,)), ((), ())), preferred_element_type=jnp.float32)
    state = state.astype(jnp.bfloat16)
    for j in range(CONTEXTS):
        mine[j] = state[16 * (j // 4) : 16 * (j // 4 + 1), 128 * (j % 4) : 128 * (j % 4 + 1)]
    to_all_contexts(lambda j: mine.at[j], theirs, state_s, state_r)
    theirs[c] = mine[c]

    scores = lax.dot_general(c_conv, b_conv, (((1,), (1,)), ((), ())), preferred_element_type=jnp.float32)
    upto = lax.broadcasted_iota(jnp.int32, (SPAN, SPAN), 0) >= lax.broadcasted_iota(jnp.int32, (SPAN, SPAN), 1)
    scores = jnp.where(upto, scores, 0.0)

    def within(h):
        gaps = jnp.minimum(columns[:, h : h + 1] - sums[h : h + 1], 0.0)
        mixing = (scores * jnp.exp(gaps) * steps[h : h + 1]).astype(jnp.bfloat16)
        here = x_conv[:, h * HEAD_DIM : (h + 1) * HEAD_DIM]
        return (
            jnp.dot(mixing, here, preferred_element_type=jnp.float32) + skip_ref[h] * here.astype(jnp.float32)
        )

    for b in range(4):
        inner[:, 128 * b : 128 * (b + 1)] = jnp.concatenate([within(2 * b), within(2 * b + 1)], 1)

    all_of(decays, decay_s, decay_r).wait_recv()
    all_of(theirs, state_s, state_r).wait_recv()
    carried = jnp.zeros((16, 128), jnp.float32)
    for j in range(CONTEXTS):
        leaving[j] = carried.astype(jnp.bfloat16)
        carried = decays[j, pl.ds(c % 4, 1)] * carried + theirs[j].astype(jnp.float32)
    to_all_contexts(lambda j: leaving.at[j], arriving, start_s, start_r)
    arriving[c] = leaving[c]
    growth = jnp.exp(spread(0))
    all_of(arriving, start_s, start_r).wait_recv()
    start = jnp.concatenate(
        [jnp.concatenate([arriving[4 * i + b] for b in range(4)], 1) for i in range(8)], 0
    )
    mixed = inner[...] + growth * jnp.dot(c_conv, start, preferred_element_type=jnp.float32)
    same_head = (
        lax.broadcasted_iota(jnp.int32, (128, 128), 0) // HEAD_DIM == lax.broadcasted_iota(jnp.int32, (128, 128), 1) // HEAD_DIM
    ).astype(jnp.bfloat16)
    for b in range(4):
        part = mixed[:, 128 * b : 128 * (b + 1)]
        square = part * part
        upper = square.astype(jnp.bfloat16)
        lower = (square - upper.astype(jnp.float32)).astype(jnp.bfloat16)
        total = jnp.dot(upper, same_head, preferred_element_type=jnp.float32) + jnp.dot(
            lower, same_head, preferred_element_type=jnp.float32
        )
        scaled = part * lax.rsqrt(total * (1.0 / HEAD_DIM) + 1e-05) * gain_ref[:, 128 * b : 128 * (b + 1)]
        out_ref[:, 128 * b : 128 * (b + 1)] = scaled.astype(jnp.bfloat16)

    for copy in dz + bz + list(tz.values()) + tx + list(wy.values()) + list(wc.values()) + dy + [dc, rim]:
        copy.wait_send()
    for condition, copy in guarded:

        @pl.when(condition)
        def _(copy=copy):
            copy.wait_send()

    all_of(decays, decay_s, decay_r).wait_send()
    all_of(mine, state_s, state_r).wait_send()
    all_of(leaving, start_s, start_r).wait_send()


def local(
    tokens, x_weight, dt_weight, bc_weight, conv_x, conv_bc, dt_bias, a_rate, d_skip, norm_gain
):
    dma = pltpu.SemaphoreType.DMA
    in_vmem = pl.BlockSpec(memory_space=pltpu.VMEM)
    in_smem = pl.BlockSpec(memory_space=pltpu.SMEM)
    anywhere = pl.BlockSpec(memory_space=pltpu.HBM)
    return pl.pallas_call(
        layer_kernel,
        out_shape=jax.ShapeDtypeStruct((SPAN, 512), jnp.bfloat16),
        in_specs=[anywhere, anywhere, in_vmem, anywhere, in_vmem, in_vmem, in_smem, in_smem, in_smem, in_vmem],
        out_specs=in_vmem,
        scratch_shapes=[
            pltpu.VMEM((16, 16, 4096), jnp.bfloat16),
            pltpu.VMEM((32, 128, 768), jnp.bfloat16),
            pltpu.VMEM((2, 4, 4, 16, 128), jnp.bfloat16),
            pltpu.VMEM((8 + SPAN, 768), jnp.float32),
            pltpu.VMEM((SPAN, 512), jnp.float32),
            pltpu.VMEM((CONTEXTS, 8, 128), jnp.float32),
            pltpu.VMEM((CONTEXTS, 16, 128), jnp.bfloat16),
            pltpu.VMEM((CONTEXTS, 16, 128), jnp.bfloat16),
            pltpu.VMEM((CONTEXTS, 16, 128), jnp.bfloat16),
            pltpu.VMEM((CONTEXTS, 16, 128), jnp.bfloat16),
            dma((3,)),
            dma((4, 2)), dma((4, 2)), dma((21,)), dma((21,)), dma((5,)), dma((4,)), dma((4,)), dma((4,)),
            dma((4, 4)), dma((4, 4)), dma((4, 4)), dma((4, 4)), dma((4,)), dma((4,)), dma((4,)), dma((4,)), dma, dma,
            dma, dma, dma, dma, dma, dma, dma, dma,
        ],
        compiler_params=pltpu.CompilerParams(collective_id=0, has_side_effects=True, vmem_limit_bytes=60 * 2**20),
        name="layer",
    )(tokens, x_weight, dt_weight.T, bc_weight, conv_x, conv_bc, dt_bias, a_rate, d_skip, norm_gain.reshape(1, 512))


def solution(mesh):
    in_specs = (
        P(("context", "tensor"), None),
        P("context", "tensor"),
        P("context", "tensor"),
        P(None, "context", None),
        P(None, "tensor"),
        P(),
        P("tensor"),
        P("tensor"),
        P("tensor"),
        P("tensor"),
    )
    out_specs = P("context", "tensor")
    return jax.shard_map(local, mesh=mesh, in_specs=in_specs, out_specs=out_specs, check_vma=False)
```

```python
import jax
import jax.numpy as jnp
from jax import lax
from jax.experimental import pallas as pl
from jax.experimental.pallas import tpu as pltpu
from jax.sharding import PartitionSpec as P

MESH = pl.DeviceIdType.MESH

HEAD_DIM = 64
STATE = 128
SPAN = 256
CONV = 4
CONTEXTS = 32
PARTS = 2
WIDE = 4096 // PARTS


def place():
    c = lax.axis_index("context")
    t = lax.axis_index("tensor")
    return t // 4, c // 8, t % 4, (c // 2) % 4, c % 2


def device(x, y, z_hi, z_lo, core):
    return ((y % 4) * 8 + (z_lo % 4) * 2 + core, (x % 4) * 4 + z_hi % 4)


def along_z(z, by):
    other = (z + by + 16) % 16
    return other // 4, other % 4


ORDER = ((0, 1, 2, 3), (1, 0, 2, 3), (2, 1, 3, 0), (3, 2, 1, 0))
ONWARD = (None, (1, 1), (-1, -1), (-1, 1))


def pick(index, values):
    out = values[-1]
    for k in range(len(values) - 2, -1, -1):
        out = jnp.where(index == k, values[k], out)
    return out


def layer_kernel(
    tok_ref, w_ref, dt_ref, bc_ref, conv_x_ref, conv_bc_ref, bias_ref, rate_ref, skip_ref, gain_ref,
    out_ref,
    dt_own, x_taps, bc_taps, bias, rate, skip, gain, small_sem,
    tok, wb, dts, pre, inner, decays, mine, theirs, leaving, arriving,
    local_sem, tz_s, tz_r, tx_s, tx_r, wz_s, wz_r, bz_s, bz_r,
    wy_s, wy_r, wc_s, wc_r, dz_s, dz_r, dy_s, dy_r, dc_s, dc_r,
    rim_s, rim_r, decay_s, decay_r, state_s, state_r, start_s, start_r,
):
    x, y, z_hi, z_lo, core = place()
    z = z_hi * 4 + z_lo
    t_own = x * 4 + z_hi
    c = lax.axis_index("context")
    t = lax.axis_index("tensor")
    sibling = device(x, y, z_hi, z_lo, 1 - core)

    def describe(src, dst, ssem, rsem, dev):
        return pltpu.make_async_remote_copy(
            src_ref=src, dst_ref=dst, send_sem=ssem, recv_sem=rsem, device_id=dev, device_id_type=MESH
        )

    def send(*args):
        copy = describe(*args)
        copy.start()
        return copy

    def piece(y_at, z_at, core_at):
        return (y_at % 4) * 8 + (z_at % 4) * 2 + core_at

    def x_part(ref, p):
        return ref.at[p, :, pl.ds(0, 512)]

    own = piece(y, z_lo, core)
    group = x * 2 + z_hi // 2
    local = [
        pltpu.make_async_copy(w_ref, x_part(wb, own), local_sem.at[1]),
        pltpu.make_async_copy(bc_ref.at[group], wb.at[own, :, pl.ds(512, 256)], local_sem.at[2]),
        pltpu.make_async_copy(tok_ref, tok.at[t_own], local_sem.at[0]),
    ]
    small = [
        pltpu.make_async_copy(src, dst, small_sem.at[i])
        for i, (src, dst) in enumerate(
            (
                (dt_ref, dt_own), (conv_x_ref, x_taps), (conv_bc_ref, bc_taps), (bias_ref, bias),
                (rate_ref, rate), (skip_ref, skip), (gain_ref, gain),
            )
        )
    ]
    for copy in local + small:
        copy.start()

    barrier = pltpu.get_barrier_semaphore()
    partners = [device(x, y, z_hi + 1, z_lo, core), device(x, y, z_hi + 3, z_lo, core), sibling]
    for by in (1, 2, 3):
        partners.append(device(x + by, y, z_hi, z_lo, core))
        partners.append(device(x, y + by, z_hi, z_lo, core))
        partners.append(device(x, y, z_hi, z_lo + by, core))
    for by in (1, -1, 2, -2):
        partners.append(device(x, y, *along_z(z, by), core))
    for by in (1, CONTEXTS - 1):
        partners.append(((c + by) % CONTEXTS, t))
    for partner in partners:
        pl.semaphore_signal(barrier, inc=1, device_id=partner, device_id_type=MESH)
    pl.semaphore_wait(barrier, len(partners))

    arrival = [pick(z_lo, [row[j] for row in ORDER]) for j in range(4)]
    guarded = []

    def rows_along_z(z_at, onward, sem, condition):
        to = (z_lo + onward + 4) % 4
        number = pick(to, [pick(z_at, [row.index(k) for k in range(4)]) for row in ORDER])
        block = x_part(wb, piece(y, z_at, core))
        copy = describe(block, block, wz_s.at[sem], wz_r.at[number], device(x, y, z_hi, to, core))

        @pl.when(condition)
        def _():
            copy.start()

        guarded.append((condition, copy))

    for copy in local[:2]:
        copy.wait()
    rows_along_z(z_lo, 1, 0, z_lo < 3)
    rows_along_z(z_lo, -1, 1, z_lo > 0)
    bz = []
    for i, (by, first, count) in enumerate(((1, 0, 128), (-1, 0, 128), (2, 0, 64), (-2, 64, 64))):
        hi, lo = along_z(z, by)
        bz.append(
            send(
                bc_ref.at[x * 2 + hi // 2, pl.ds(first, count)],
                wb.at[own, pl.ds(first, count), pl.ds(512, 256)],
                bz_s.at[i], bz_r.at[i], device(x, y, hi, lo, core),
            )
        )
    small[0].wait()
    dts[core, y, z_lo] = jnp.concatenate(
        [dt_own[...].astype(jnp.float32), jnp.zeros((8, 128), jnp.float32)], 0
    ).astype(jnp.bfloat16)
    block = dts.at[core, y, z_lo]
    dz = [send(block, block, dz_s.at[by], dz_r.at[by], device(x, y, z_hi, z_lo + by, core)) for by in (1, 2, 3)]

    wy = {}
    wc = {}

    def to_sibling(j, by):
        slot = wb.at[piece(y + by, arrival[j], core)]
        wc[j, by] = send(slot, slot, wc_s.at[j, by], wc_r.at[j, by], sibling)

    def rows_along_y(j):
        slot = wb.at[piece(y, arrival[j], core)]
        wy[j, 0] = send(slot, slot, wy_s.at[j, 0], wy_r.at[j, 0], device(x, y + 1, z_hi, z_lo, core))
        wy[j, 1] = send(slot, slot, wy_s.at[j, 1], wy_r.at[j, 1], device(x, y + 3, z_hi, z_lo, core))
        to_sibling(j, 0)

    def next_rows(j):
        block = x_part(wb, piece(y, arrival[j], core))
        describe(block, block, wz_s.at[0], wz_r.at[j], sibling).wait_recv()
        rows_along_z(arrival[j], jnp.where(z_lo == 1, *ONWARD[j]), 1 + j, (z_lo == 1) | (z_lo == 2))
        rows_along_y(j)

    def relay_along_y(j):
        wy[j, 0].wait_recv()
        half = wb.at[piece(y + 3, arrival[j], core), pl.ds(0, 64)]
        wy[j, 2] = send(half, half, wy_s.at[j, 2], wy_r.at[j, 2], device(x, y + 1, z_hi, z_lo, core))
        wy[j, 1].wait_recv()
        half = wb.at[piece(y + 1, arrival[j], core), pl.ds(64, 64)]
        wy[j, 3] = send(half, half, wy_s.at[j, 3], wy_r.at[j, 3], device(x, y + 3, z_hi, z_lo, core))
        to_sibling(j, 3)
        to_sibling(j, 1)

    def last_along_y(j):
        wy[j, 2].wait_recv()
        wy[j, 3].wait_recv()
        to_sibling(j, 2)

    tx = {}
    tz = {}

    def tokens_along_x(k, hi, part):
        slot = tok.at[x * 4 + hi % 4, :, columns_of(part)]
        for i, by in enumerate((1, 3, 2)):
            tx[k, part, by] = send(
                slot, slot, tx_s.at[k, part, i], tx_r.at[k, part, i], device(x + by, y, z_hi, z_lo, core)
            )

    def columns_of(part):
        return pl.ds(part * WIDE, WIDE)

    up, down = device(x, y, z_hi + 1, z_lo, core), device(x, y, z_hi + 3, z_lo, core)

    def tokens_along_z():
        for part in range(PARTS):
            block = tok.at[t_own, :, columns_of(part)]
            tz[0, part] = send(block, block, tz_s.at[0, part], tz_r.at[0, part], up)
            tz[1, part] = send(block, block, tz_s.at[1, part], tz_r.at[1, part], down)

    def relay_tokens(part):
        tz[0, part].wait_recv()
        block = tok.at[x * 4 + (z_hi + 3) % 4, :, pl.ds(part * WIDE, WIDE // 2)]
        tz[2, part] = send(block, block, tz_s.at[2, part], tz_r.at[2, part], up)
        tz[1, part].wait_recv()
        block = tok.at[x * 4 + (z_hi + 1) % 4, :, pl.ds(part * WIDE + WIDE // 2, WIDE // 2)]
        tz[3, part] = send(block, block, tz_s.at[3, part], tz_r.at[3, part], down)
        tokens_along_x(1, z_hi + 3, part)
        tokens_along_x(2, z_hi + 1, part)

    def last_tokens(part):
        tz[2, part].wait_recv()
        tz[3, part].wait_recv()
        tokens_along_x(3, z_hi + 2, part)

    rows_along_y(0)
    local[2].wait()
    for part in range(PARTS):
        tokens_along_x(0, z_hi, part)
    tokens_along_z()
    for copy in dz:
        copy.wait_recv()
    block = dts.at[core, y]
    dy = [
        send(block, block, dy_s.at[by], dy_r.at[by], device(x, y + by, z_hi, z_lo, core)) for by in (1, 2, 3)
    ]
    for copy in bz:
        copy.wait_recv()
    next_rows(1)
    next_rows(2)
    relay_tokens(0)
    relay_along_y(0)
    for copy in dy:
        copy.wait_recv()
    block = dts.at[core]
    dc = send(block, block, dc_s, dc_r, sibling)
    next_rows(3)
    relay_tokens(1)
    relay_along_y(1)
    last_tokens(0)
    relay_along_y(2)
    relay_along_y(3)
    last_tokens(1)
    for j in range(4):
        last_along_y(j)
    dc.wait_recv()
    for copy in wc.values():
        copy.wait_recv()

    def to_all_contexts(source, slots, ssem, rsem):
        def one(step, carry):
            j = (c + step) % CONTEXTS
            send(source(j), slots.at[c], ssem, rsem, (j, t))
            return carry

        lax.fori_loop(1, CONTEXTS, one, 0)

    def all_of(slots, ssem, rsem):
        several = slots.at[pl.ds(0, CONTEXTS - 1)]
        return describe(several, several, ssem, rsem, sibling)

    for copy in small[1:]:
        copy.wait()
    both = jnp.zeros((SPAN, 768), jnp.float32)
    dt_raw = jnp.zeros((SPAN, 16), jnp.float32)
    count = CONTEXTS // PARTS
    for part in range(PARTS):
        for (_, at, _), copy in tx.items():
            if at == part:
                copy.wait_recv()
        some = tok[:, :, part * WIDE : (part + 1) * WIDE].reshape(SPAN, WIDE)
        pieces = range(part * count, (part + 1) * count)
        both += jnp.dot(
            some, wb[part * count : (part + 1) * count].reshape(WIDE, 768), preferred_element_type=jnp.float32
        )
        dt_cols = jnp.concatenate([dts[p % 2, p // 8, (p // 2) % 4] for p in pieces], 1)
        dt_raw += lax.dot_general(some, dt_cols, (((1,), (1,)), ((), ())), preferred_element_type=jnp.float32)
    pre[8:] = both.astype(jnp.bfloat16).astype(jnp.float32)
    rim = send(
        pre.at[pl.ds(SPAN, 8)], pre.at[pl.ds(0, 8)], rim_s, rim_r, ((c + 1) % CONTEXTS, t)
    )
    raw = jnp.concatenate([dt_raw, jnp.zeros((SPAN, 112), jnp.float32)], 1).T[:8]
    diagonal = lax.broadcasted_iota(jnp.int32, (8, 8), 0) == lax.broadcasted_iota(jnp.int32, (8, 8), 1)

    def per_head(ref):
        return jnp.sum(jnp.where(diagonal, jnp.broadcast_to(ref[...], (8, 8)), 0.0), axis=1, keepdims=True)

    raw = raw + per_head(bias)
    steps = jnp.maximum(raw, 0.0) + jnp.log1p(jnp.exp(-jnp.abs(raw)))
    upto = lax.broadcasted_iota(jnp.int32, (SPAN, SPAN), 0) <= lax.broadcasted_iota(jnp.int32, (SPAN, SPAN), 1)
    sums = jnp.dot(
        -per_head(rate) * steps, upto.astype(jnp.float32),
        precision=lax.Precision.HIGHEST, preferred_element_type=jnp.float32,
    )
    last = jnp.broadcast_to(sums[:, SPAN - 1 :], (8, SPAN))
    tails = jnp.exp(last - sums) * steps
    columns = jnp.concatenate([sums, tails, jnp.zeros((112, SPAN), jnp.float32)], 0).T
    low_lanes = lax.broadcasted_iota(jnp.int32, (1, 128), 1) < HEAD_DIM
    whole = jnp.exp(last[:, :128])
    decays[c] = jnp.concatenate(
        [jnp.where(low_lanes, whole[2 * b : 2 * b + 1], whole[2 * b + 1 : 2 * b + 2]) for b in range(4)]
        + [jnp.zeros((4, 128), jnp.float32)],
        0,
    )
    to_all_contexts(lambda j: decays.at[c], decays, decay_s, decay_r)

    def spread(first):
        return jnp.concatenate(
            [
                jnp.where(low_lanes, columns[:, first + 2 * b : first + 2 * b + 1], columns[:, first + 2 * b + 1 : first + 2 * b + 2])
                for b in range(4)
            ],
            1,
        )


    x_tap = x_taps[...].astype(jnp.float32)
    bc_tap = bc_taps[group].astype(jnp.float32)

    def convolved(first, width, taps, start, count):
        total = sum(
            taps[k : k + 1] * pre[start + 5 + k : start + 5 + k + count, first : first + width] for k in range(CONV)
        )
        return total / (1.0 + jnp.exp(-total))

    later = (
        convolved(0, 512, x_tap, 8, SPAN - 8),
        convolved(512, 256, bc_tap, 8, SPAN - 8),
    )
    rim.wait_recv()

    @pl.when(c == 0)
    def _():
        pre[:8] = jnp.zeros((8, 768), jnp.float32)

    earlier = (convolved(0, 512, x_tap, 0, 8), convolved(512, 256, bc_tap, 0, 8))
    x_conv, bc_conv = (
        jnp.concatenate(pair, 0).astype(jnp.bfloat16) for pair in zip(earlier, later)
    )
    b_conv, c_conv = bc_conv[:, :STATE], bc_conv[:, STATE:]

    weighted = (x_conv.astype(jnp.float32) * spread(8)).astype(jnp.bfloat16)
    state = lax.dot_general(b_conv, weighted, (((0,), (0,)), ((), ())), preferred_element_type=jnp.float32)
    state = state.astype(jnp.bfloat16)
    for j in range(CONTEXTS):
        mine[j] = state[16 * (j // 4) : 16 * (j // 4 + 1), 128 * (j % 4) : 128 * (j % 4 + 1)]
    to_all_contexts(lambda j: mine.at[j], theirs, state_s, state_r)
    theirs[c] = mine[c]

    scores = lax.dot_general(c_conv, b_conv, (((1,), (1,)), ((), ())), preferred_element_type=jnp.float32)
    upto = lax.broadcasted_iota(jnp.int32, (SPAN, SPAN), 0) >= lax.broadcasted_iota(jnp.int32, (SPAN, SPAN), 1)
    scores = jnp.where(upto, scores, 0.0)

    def within(h):
        gaps = jnp.minimum(columns[:, h : h + 1] - sums[h : h + 1], 0.0)
        mixing = (scores * jnp.exp(gaps) * steps[h : h + 1]).astype(jnp.bfloat16)
        here = x_conv[:, h * HEAD_DIM : (h + 1) * HEAD_DIM]
        return (
            jnp.dot(mixing, here, preferred_element_type=jnp.float32) + skip[:, h : h + 1] * here.astype(jnp.float32)
        )

    for b in range(4):
        inner[:, 128 * b : 128 * (b + 1)] = jnp.concatenate([within(2 * b), within(2 * b + 1)], 1)

    all_of(decays, decay_s, decay_r).wait_recv()
    all_of(theirs, state_s, state_r).wait_recv()
    carried = jnp.zeros((16, 128), jnp.float32)
    for j in range(CONTEXTS):
        leaving[j] = carried.astype(jnp.bfloat16)
        carried = decays[j, pl.ds(c % 4, 1)] * carried + theirs[j].astype(jnp.float32)
    to_all_contexts(lambda j: leaving.at[j], arriving, start_s, start_r)
    arriving[c] = leaving[c]
    growth = jnp.exp(spread(0))
    all_of(arriving, start_s, start_r).wait_recv()
    start = jnp.concatenate(
        [jnp.concatenate([arriving[4 * i + b] for b in range(4)], 1) for i in range(8)], 0
    )
    mixed = inner[...] + growth * jnp.dot(c_conv, start, preferred_element_type=jnp.float32)
    same_head = (
        lax.broadcasted_iota(jnp.int32, (128, 128), 0) // HEAD_DIM == lax.broadcasted_iota(jnp.int32, (128, 128), 1) // HEAD_DIM
    ).astype(jnp.bfloat16)
    for b in range(4):
        part = mixed[:, 128 * b : 128 * (b + 1)]
        square = part * part
        upper = square.astype(jnp.bfloat16)
        lower = (square - upper.astype(jnp.float32)).astype(jnp.bfloat16)
        total = jnp.dot(upper, same_head, preferred_element_type=jnp.float32) + jnp.dot(
            lower, same_head, preferred_element_type=jnp.float32
        )
        scaled = part * lax.rsqrt(total * (1.0 / HEAD_DIM) + 1e-05) * gain[:, 128 * b : 128 * (b + 1)]
        out_ref[:, 128 * b : 128 * (b + 1)] = scaled.astype(jnp.bfloat16)

    for copy in dz + bz + list(tz.values()) + list(tx.values()) + list(wy.values()) + list(wc.values()) + dy + [dc, rim]:
        copy.wait_send()
    for condition, copy in guarded:

        @pl.when(condition)
        def _(copy=copy):
            copy.wait_send()

    all_of(decays, decay_s, decay_r).wait_send()
    all_of(mine, state_s, state_r).wait_send()
    all_of(leaving, start_s, start_r).wait_send()


def local(
    tokens, x_weight, dt_weight, bc_weight, conv_x, conv_bc, dt_bias, a_rate, d_skip, norm_gain
):
    dma = pltpu.SemaphoreType.DMA
    in_vmem = pl.BlockSpec(memory_space=pltpu.VMEM)
    anywhere = pl.BlockSpec(memory_space=pltpu.HBM)
    return pl.pallas_call(
        layer_kernel,
        out_shape=jax.ShapeDtypeStruct((SPAN, 512), jnp.bfloat16),
        in_specs=[anywhere] * 10,
        out_specs=in_vmem,
        scratch_shapes=[
            pltpu.VMEM((8, 128), jnp.bfloat16),
            pltpu.VMEM((4, 512), jnp.bfloat16),
            pltpu.VMEM((8, 4, 256), jnp.bfloat16),
            pltpu.VMEM((1, 8), jnp.float32),
            pltpu.VMEM((1, 8), jnp.float32),
            pltpu.VMEM((1, 8), jnp.float32),
            pltpu.VMEM((1, 512), jnp.float32),
            dma((7,)),
            pltpu.VMEM((16, 16, 4096), jnp.bfloat16),
            pltpu.VMEM((32, 128, 768), jnp.bfloat16),
            pltpu.VMEM((2, 4, 4, 16, 128), jnp.bfloat16),
            pltpu.VMEM((8 + SPAN, 768), jnp.float32),
            pltpu.VMEM((SPAN, 512), jnp.float32),
            pltpu.VMEM((CONTEXTS, 8, 128), jnp.float32),
            pltpu.VMEM((CONTEXTS, 16, 128), jnp.bfloat16),
            pltpu.VMEM((CONTEXTS, 16, 128), jnp.bfloat16),
            pltpu.VMEM((CONTEXTS, 16, 128), jnp.bfloat16),
            pltpu.VMEM((CONTEXTS, 16, 128), jnp.bfloat16),
            dma((3,)),
            dma((4, PARTS)), dma((4, PARTS)), dma((4, PARTS, 3)), dma((4, PARTS, 3)), dma((5,)), dma((4,)), dma((4,)), dma((4,)),
            dma((4, 4)), dma((4, 4)), dma((4, 4)), dma((4, 4)), dma((4,)), dma((4,)), dma((4,)), dma((4,)), dma, dma,
            dma, dma, dma, dma, dma, dma, dma, dma,
        ],
        compiler_params=pltpu.CompilerParams(collective_id=0, has_side_effects=True, vmem_limit_bytes=60 * 2**20),
        name="layer",
    )(tokens, x_weight, dt_weight.T, bc_weight, conv_x, conv_bc,
      dt_bias.reshape(1, 8), a_rate.reshape(1, 8), d_skip.reshape(1, 8), norm_gain.reshape(1, 512))


def solution(mesh):
    in_specs = (
        P(("context", "tensor"), None),
        P("context", "tensor"),
        P("context", "tensor"),
        P(None, "context", None),
        P(None, "tensor"),
        P(),
        P("tensor"),
        P("tensor"),
        P("tensor"),
        P("tensor"),
    )
    out_specs = P("context", "tensor")
    return jax.shard_map(local, mesh=mesh, in_specs=in_specs, out_specs=out_specs, check_vma=False)
```

```python
import jax
import jax.numpy as jnp
from jax import lax
from jax.experimental import pallas as pl
from jax.experimental.pallas import tpu as pltpu
from jax.sharding import PartitionSpec as P

MESH = pl.DeviceIdType.MESH

HEAD_DIM = 64
STATE = 128
SPAN = 256
CONV = 4
CONTEXTS = 32
OWNERS = 16
PARTS = 2
WIDE = 4096 // PARTS


def place():
    c = lax.axis_index("context")
    t = lax.axis_index("tensor")
    return t // 4, c // 8, t % 4, (c // 2) % 4, c % 2


def device(x, y, z_hi, z_lo, core):
    return ((y % 4) * 8 + (z_lo % 4) * 2 + core, (x % 4) * 4 + z_hi % 4)


def along_z(z, by):
    other = (z + by + 16) % 16
    return other // 4, other % 4


ORDER = ((0, 1, 2, 3), (1, 0, 2, 3), (2, 1, 3, 0), (3, 2, 1, 0))
ONWARD = (None, (1, 1), (-1, -1), (-1, 1))


def pick(index, values):
    out = values[-1]
    for k in range(len(values) - 2, -1, -1):
        out = jnp.where(index == k, values[k], out)
    return out


def layer_kernel(
    tok_ref, w_ref, dt_ref, bc_ref, conv_x_ref, conv_bc_ref, bias_ref, rate_ref, skip_ref, gain_ref,
    out_ref,
    dt_own, x_taps, bc_taps, bias, rate, skip, gain, small_sem,
    tok, wb, dts, pre, inner, decays, mine, theirs, leaving, arriving,
    local_sem, tz_s, tz_r, tx_s, tx_r, wz_s, wz_r, bz_s, bz_r,
    wy_s, wy_r, wc_s, wc_r, dz_s, dz_r, dy_s, dy_r, dc_s, dc_r,
    rim_s, rim_r, decay_s, decay_r, state_s, state_r, start_s, start_r,
):
    x, y, z_hi, z_lo, core = place()
    z = z_hi * 4 + z_lo
    t_own = x * 4 + z_hi
    c = lax.axis_index("context")
    t = lax.axis_index("tensor")
    sibling = device(x, y, z_hi, z_lo, 1 - core)

    def describe(src, dst, ssem, rsem, dev):
        return pltpu.make_async_remote_copy(
            src_ref=src, dst_ref=dst, send_sem=ssem, recv_sem=rsem, device_id=dev, device_id_type=MESH
        )

    def send(*args):
        copy = describe(*args)
        copy.start()
        return copy

    def piece(y_at, z_at, core_at):
        return (y_at % 4) * 8 + (z_at % 4) * 2 + core_at

    def x_part(ref, p):
        return ref.at[p, :, pl.ds(0, 512)]

    own = piece(y, z_lo, core)
    group = x * 2 + z_hi // 2
    local = [
        pltpu.make_async_copy(w_ref, x_part(wb, own), local_sem.at[1]),
        pltpu.make_async_copy(bc_ref.at[group], wb.at[own, :, pl.ds(512, 256)], local_sem.at[2]),
        pltpu.make_async_copy(tok_ref, tok.at[t_own], local_sem.at[0]),
    ]
    small = [
        pltpu.make_async_copy(src, dst, small_sem.at[i])
        for i, (src, dst) in enumerate(
            (
                (dt_ref, dt_own), (conv_x_ref, x_taps), (conv_bc_ref, bc_taps), (bias_ref, bias),
                (rate_ref, rate), (skip_ref, skip), (gain_ref, gain),
            )
        )
    ]
    for copy in local + small:
        copy.start()

    barrier = pltpu.get_barrier_semaphore()
    partners = [device(x, y, z_hi + 1, z_lo, core), device(x, y, z_hi + 3, z_lo, core), sibling]
    for by in (1, 2, 3):
        partners.append(device(x + by, y, z_hi, z_lo, core))
        partners.append(device(x, y + by, z_hi, z_lo, core))
        partners.append(device(x, y, z_hi, z_lo + by, core))
    for by in (1, -1, 2, -2):
        partners.append(device(x, y, *along_z(z, by), core))
    for by in (1, CONTEXTS - 1):
        partners.append(((c + by) % CONTEXTS, t))
    for partner in partners:
        pl.semaphore_signal(barrier, inc=1, device_id=partner, device_id_type=MESH)
    pl.semaphore_wait(barrier, len(partners))

    arrival = [pick(z_lo, [row[j] for row in ORDER]) for j in range(4)]
    guarded = []

    def rows_along_z(z_at, onward, sem, condition):
        to = (z_lo + onward + 4) % 4
        number = pick(to, [pick(z_at, [row.index(k) for k in range(4)]) for row in ORDER])
        block = x_part(wb, piece(y, z_at, core))
        copy = describe(block, block, wz_s.at[sem], wz_r.at[number], device(x, y, z_hi, to, core))

        @pl.when(condition)
        def _():
            copy.start()

        guarded.append((condition, copy))

    for copy in local[:2]:
        copy.wait()
    rows_along_z(z_lo, 1, 0, z_lo < 3)
    rows_along_z(z_lo, -1, 1, z_lo > 0)
    bz = []
    for i, (by, first, count) in enumerate(((1, 0, 128), (-1, 0, 128), (2, 0, 64), (-2, 64, 64))):
        hi, lo = along_z(z, by)
        bz.append(
            send(
                bc_ref.at[x * 2 + hi // 2, pl.ds(first, count)],
                wb.at[own, pl.ds(first, count), pl.ds(512, 256)],
                bz_s.at[i], bz_r.at[i], device(x, y, hi, lo, core),
            )
        )
    small[0].wait()
    dts[core, y, z_lo] = jnp.concatenate(
        [dt_own[...].astype(jnp.float32), jnp.zeros((8, 128), jnp.float32)], 0
    ).astype(jnp.bfloat16)
    block = dts.at[core, y, z_lo]
    dz = [send(block, block, dz_s.at[by], dz_r.at[by], device(x, y, z_hi, z_lo + by, core)) for by in (1, 2, 3)]

    wy = {}
    wc = {}

    def to_sibling(j, by):
        slot = wb.at[piece(y + by, arrival[j], core)]
        wc[j, by] = send(slot, slot, wc_s.at[j, by], wc_r.at[j, by], sibling)

    def rows_along_y(j):
        slot = wb.at[piece(y, arrival[j], core)]
        wy[j, 0] = send(slot, slot, wy_s.at[j, 0], wy_r.at[j, 0], device(x, y + 1, z_hi, z_lo, core))
        wy[j, 1] = send(slot, slot, wy_s.at[j, 1], wy_r.at[j, 1], device(x, y + 3, z_hi, z_lo, core))
        to_sibling(j, 0)

    def next_rows(j):
        block = x_part(wb, piece(y, arrival[j], core))
        describe(block, block, wz_s.at[0], wz_r.at[j], sibling).wait_recv()
        rows_along_z(arrival[j], jnp.where(z_lo == 1, *ONWARD[j]), 1 + j, (z_lo == 1) | (z_lo == 2))
        rows_along_y(j)

    def relay_along_y(j):
        wy[j, 0].wait_recv()
        half = wb.at[piece(y + 3, arrival[j], core), pl.ds(0, 64)]
        wy[j, 2] = send(half, half, wy_s.at[j, 2], wy_r.at[j, 2], device(x, y + 1, z_hi, z_lo, core))
        wy[j, 1].wait_recv()
        half = wb.at[piece(y + 1, arrival[j], core), pl.ds(64, 64)]
        wy[j, 3] = send(half, half, wy_s.at[j, 3], wy_r.at[j, 3], device(x, y + 3, z_hi, z_lo, core))
        to_sibling(j, 3)
        to_sibling(j, 1)

    def last_along_y(j):
        wy[j, 2].wait_recv()
        wy[j, 3].wait_recv()
        to_sibling(j, 2)

    tx = {}
    tz = {}

    def tokens_along_x(k, hi, part, columns=None):
        slot = tok.at[x * 4 + hi % 4, :, columns_of(part) if columns is None else columns]
        for i, by in enumerate((1, 3, 2)):
            tx[k, part, by] = send(
                slot, slot, tx_s.at[k, part, i], tx_r.at[k, part, i], device(x + by, y, z_hi, z_lo, core)
            )

    def columns_of(part):
        return pl.ds(part * WIDE, WIDE)

    up, down = device(x, y, z_hi + 1, z_lo, core), device(x, y, z_hi + 3, z_lo, core)

    def tokens_along_z():
        for part in range(PARTS):
            block = tok.at[t_own, :, columns_of(part)]
            tz[0, part] = send(block, block, tz_s.at[0, part], tz_r.at[0, part], up)
            tz[1, part] = send(block, block, tz_s.at[1, part], tz_r.at[1, part], down)

    def relay_tokens(part):
        tz[0, part].wait_recv()
        block = tok.at[x * 4 + (z_hi + 3) % 4, :, pl.ds(part * WIDE, WIDE // 2)]
        tz[2, part] = send(block, block, tz_s.at[2, part], tz_r.at[2, part], up)
        tz[1, part].wait_recv()
        block = tok.at[x * 4 + (z_hi + 1) % 4, :, pl.ds(part * WIDE + WIDE // 2, WIDE // 2)]
        tz[3, part] = send(block, block, tz_s.at[3, part], tz_r.at[3, part], down)
        tokens_along_x(1, z_hi + 3, part)
        tokens_along_x(2, z_hi + 1, part)

    def last_tokens(part):
        tz[2, part].wait_recv()
        tz[3, part].wait_recv()
        tokens_along_x(3, z_hi + 2, part)

    rows_along_y(0)
    local[2].wait()
    tokens_along_x(0, z_hi, 0, pl.ds(0, 4096))
    tokens_along_z()
    for copy in dz:
        copy.wait_recv()
    block = dts.at[core, y]
    dy = [
        send(block, block, dy_s.at[by], dy_r.at[by], device(x, y + by, z_hi, z_lo, core)) for by in (1, 2, 3)
    ]
    nearer = jnp.where(z_lo == 0, 1, 0)

    def neighbour_rows(which):
        slot = wb.at[own, :, pl.ds(512, 256)]
        describe(slot, slot, bz_s.at[0], bz_r.at[which], sibling).wait_recv()

    neighbour_rows(nearer)
    next_rows(1)
    neighbour_rows(1 - nearer)
    for copy in bz[2:]:
        copy.wait_recv()
    next_rows(2)
    relay_tokens(0)
    relay_along_y(0)
    for copy in dy:
        copy.wait_recv()
    block = dts.at[core]
    dc = send(block, block, dc_s, dc_r, sibling)
    next_rows(3)
    relay_tokens(1)
    relay_along_y(1)
    last_tokens(0)
    relay_along_y(2)
    relay_along_y(3)
    last_tokens(1)
    for j in range(4):
        last_along_y(j)
    dc.wait_recv()
    for copy in wc.values():
        copy.wait_recv()

    owner = (z_lo == 1) | (z_lo == 2)
    nearest = y * 4 + (z_lo // 2) * 2 + core

    def context_of(o):
        return (o // 4) * 8 + (1 + (o // 2) % 2) * 2 + o % 2

    def to_owners(source, slots, ssem, rsem):
        def one(step, carry):
            o = (nearest + step) % OWNERS
            send(source(o), slots.at[c], ssem, rsem, (context_of(o), t))
            return carry

        @pl.when(~owner)
        def _():
            one(0, 0)

        lax.fori_loop(1, OWNERS, one, 0)

    def several(slots, count, ssem, rsem):
        some = slots.at[pl.ds(0, count)]
        return describe(some, some, ssem, rsem, sibling)

    for copy in small[1:]:
        copy.wait()
    both = jnp.zeros((SPAN, 768), jnp.float32)
    dt_raw = jnp.zeros((SPAN, 16), jnp.float32)
    count = CONTEXTS // PARTS
    for part in range(PARTS):
        for (_, at, _), copy in tx.items():
            if at == part:
                copy.wait_recv()
        some = tok[:, :, part * WIDE : (part + 1) * WIDE].reshape(SPAN, WIDE)
        pieces = range(part * count, (part + 1) * count)
        both += jnp.dot(
            some, wb[part * count : (part + 1) * count].reshape(WIDE, 768), preferred_element_type=jnp.float32
        )
        dt_cols = jnp.concatenate([dts[p % 2, p // 8, (p // 2) % 4] for p in pieces], 1)
        dt_raw += lax.dot_general(some, dt_cols, (((1,), (1,)), ((), ())), preferred_element_type=jnp.float32)
    pre[8:] = both.astype(jnp.bfloat16).astype(jnp.float32)
    rim = send(
        pre.at[pl.ds(SPAN, 8)], pre.at[pl.ds(0, 8)], rim_s, rim_r, ((c + 1) % CONTEXTS, t)
    )
    raw = jnp.concatenate([dt_raw, jnp.zeros((SPAN, 112), jnp.float32)], 1).T[:8]
    diagonal = lax.broadcasted_iota(jnp.int32, (8, 8), 0) == lax.broadcasted_iota(jnp.int32, (8, 8), 1)

    def per_head(ref):
        return jnp.sum(jnp.where(diagonal, jnp.broadcast_to(ref[...], (8, 8)), 0.0), axis=1, keepdims=True)

    raw = raw + per_head(bias)
    steps = jnp.maximum(raw, 0.0) + jnp.log1p(jnp.exp(-jnp.abs(raw)))
    upto = lax.broadcasted_iota(jnp.int32, (SPAN, SPAN), 0) <= lax.broadcasted_iota(jnp.int32, (SPAN, SPAN), 1)
    sums = jnp.dot(
        -per_head(rate) * steps, upto.astype(jnp.float32),
        precision=lax.Precision.HIGHEST, preferred_element_type=jnp.float32,
    )
    last = jnp.broadcast_to(sums[:, SPAN - 1 :], (8, SPAN))
    tails = jnp.exp(last - sums) * steps
    columns = jnp.concatenate([sums, tails, jnp.zeros((112, SPAN), jnp.float32)], 0).T
    low_lanes = lax.broadcasted_iota(jnp.int32, (1, 128), 1) < HEAD_DIM
    whole = jnp.exp(last[:, :128])
    decays[c] = jnp.concatenate(
        [jnp.where(low_lanes, whole[2 * b : 2 * b + 1], whole[2 * b + 1 : 2 * b + 2]) for b in range(4)]
        + [jnp.zeros((4, 128), jnp.float32)],
        0,
    )
    to_owners(lambda o: decays.at[c], decays, decay_s, decay_r)

    def spread(first):
        return jnp.concatenate(
            [
                jnp.where(low_lanes, columns[:, first + 2 * b : first + 2 * b + 1], columns[:, first + 2 * b + 1 : first + 2 * b + 2])
                for b in range(4)
            ],
            1,
        )


    x_tap = x_taps[...].astype(jnp.float32)
    bc_tap = bc_taps[group].astype(jnp.float32)

    def convolved(first, width, taps, start, count):
        total = sum(
            taps[k : k + 1] * pre[start + 5 + k : start + 5 + k + count, first : first + width] for k in range(CONV)
        )
        return total / (1.0 + jnp.exp(-total))

    later = (
        convolved(0, 512, x_tap, 8, SPAN - 8),
        convolved(512, 256, bc_tap, 8, SPAN - 8),
    )
    rim.wait_recv()

    @pl.when(c == 0)
    def _():
        pre[:8] = jnp.zeros((8, 768), jnp.float32)

    earlier = (convolved(0, 512, x_tap, 0, 8), convolved(512, 256, bc_tap, 0, 8))
    x_conv, bc_conv = (
        jnp.concatenate(pair, 0).astype(jnp.bfloat16) for pair in zip(earlier, later)
    )
    b_conv, c_conv = bc_conv[:, :STATE], bc_conv[:, STATE:]

    weighted = (x_conv.astype(jnp.float32) * spread(8)).astype(jnp.bfloat16)
    state = lax.dot_general(b_conv, weighted, (((0,), (0,)), ((), ())), preferred_element_type=jnp.float32)
    state = state.astype(jnp.bfloat16)
    for o in range(OWNERS):
        for k in range(2):
            b = 2 * (o % 2) + k
            mine[o, k] = state[16 * (o // 2) : 16 * (o // 2 + 1), 128 * b : 128 * (b + 1)]
    to_owners(lambda o: mine.at[o], theirs, state_s, state_r)
    theirs[c] = mine[nearest]

    scores = lax.dot_general(c_conv, b_conv, (((1,), (1,)), ((), ())), preferred_element_type=jnp.float32)
    upto = lax.broadcasted_iota(jnp.int32, (SPAN, SPAN), 0) >= lax.broadcasted_iota(jnp.int32, (SPAN, SPAN), 1)
    scores = jnp.where(upto, scores, 0.0)

    def within(h):
        gaps = jnp.minimum(columns[:, h : h + 1] - sums[h : h + 1], 0.0)
        mixing = (scores * jnp.exp(gaps) * steps[h : h + 1]).astype(jnp.bfloat16)
        here = x_conv[:, h * HEAD_DIM : (h + 1) * HEAD_DIM]
        return (
            jnp.dot(mixing, here, preferred_element_type=jnp.float32) + skip[:, h : h + 1] * here.astype(jnp.float32)
        )

    for b in range(4):
        inner[:, 128 * b : 128 * (b + 1)] = jnp.concatenate([within(2 * b), within(2 * b + 1)], 1)

    @pl.when(owner)
    def _():
        several(decays, CONTEXTS - 1, decay_s, decay_r).wait_recv()
        several(theirs, CONTEXTS - 1, state_s, state_r).wait_recv()
        carried = jnp.zeros((2, 16, 128), jnp.float32)
        for j in range(CONTEXTS):
            leaving[j] = carried.astype(jnp.bfloat16)
            decay = decays[j, pl.ds(2 * core, 2)].reshape(2, 1, 128)
            carried = decay * carried + theirs[j].astype(jnp.float32)

        def one(step, carry):
            j = (c + step) % CONTEXTS
            send(leaving.at[j], arriving.at[nearest], start_s, start_r, (j, t))
            return carry

        lax.fori_loop(1, CONTEXTS, one, 0)
        arriving[nearest] = leaving[c]

    growth = jnp.exp(spread(0))

    @pl.when(owner)
    def _():
        several(arriving, OWNERS - 1, start_s, start_r).wait_recv()

    @pl.when(~owner)
    def _():
        several(arriving, OWNERS, start_s, start_r).wait_recv()

    start = jnp.concatenate(
        [jnp.concatenate([arriving[2 * i + b // 2, b % 2] for b in range(4)], 1) for i in range(8)], 0
    )
    mixed = inner[...] + growth * jnp.dot(c_conv, start, preferred_element_type=jnp.float32)
    same_head = (
        lax.broadcasted_iota(jnp.int32, (128, 128), 0) // HEAD_DIM == lax.broadcasted_iota(jnp.int32, (128, 128), 1) // HEAD_DIM
    ).astype(jnp.bfloat16)
    for b in range(4):
        part = mixed[:, 128 * b : 128 * (b + 1)]
        square = part * part
        upper = square.astype(jnp.bfloat16)
        lower = (square - upper.astype(jnp.float32)).astype(jnp.bfloat16)
        total = jnp.dot(upper, same_head, preferred_element_type=jnp.float32) + jnp.dot(
            lower, same_head, preferred_element_type=jnp.float32
        )
        scaled = part * lax.rsqrt(total * (1.0 / HEAD_DIM) + 1e-05) * gain[:, 128 * b : 128 * (b + 1)]
        out_ref[:, 128 * b : 128 * (b + 1)] = scaled.astype(jnp.bfloat16)

    for copy in dz + bz + list(tz.values()) + list(tx.values()) + list(wy.values()) + list(wc.values()) + dy + [dc, rim]:
        copy.wait_send()
    for condition, copy in guarded:

        @pl.when(condition)
        def _(copy=copy):
            copy.wait_send()


    @pl.when(owner)
    def _():
        several(decays, OWNERS - 1, decay_s, decay_r).wait_send()
        several(mine, OWNERS - 1, state_s, state_r).wait_send()
        several(leaving, CONTEXTS - 1, start_s, start_r).wait_send()

    @pl.when(~owner)
    def _():
        several(decays, OWNERS, decay_s, decay_r).wait_send()
        several(mine, OWNERS, state_s, state_r).wait_send()


def local(
    tokens, x_weight, dt_weight, bc_weight, conv_x, conv_bc, dt_bias, a_rate, d_skip, norm_gain
):
    dma = pltpu.SemaphoreType.DMA
    in_vmem = pl.BlockSpec(memory_space=pltpu.VMEM)
    anywhere = pl.BlockSpec(memory_space=pltpu.HBM)
    return pl.pallas_call(
        layer_kernel,
        out_shape=jax.ShapeDtypeStruct((SPAN, 512), jnp.bfloat16),
        in_specs=[anywhere] * 10,
        out_specs=in_vmem,
        scratch_shapes=[
            pltpu.VMEM((8, 128), jnp.bfloat16),
            pltpu.VMEM((4, 512), jnp.bfloat16),
            pltpu.VMEM((8, 4, 256), jnp.bfloat16),
            pltpu.VMEM((1, 8), jnp.float32),
            pltpu.VMEM((1, 8), jnp.float32),
            pltpu.VMEM((1, 8), jnp.float32),
            pltpu.VMEM((1, 512), jnp.float32),
            dma((7,)),
            pltpu.VMEM((16, 16, 4096), jnp.bfloat16),
            pltpu.VMEM((32, 128, 768), jnp.bfloat16),
            pltpu.VMEM((2, 4, 4, 16, 128), jnp.bfloat16),
            pltpu.VMEM((8 + SPAN, 768), jnp.float32),
            pltpu.VMEM((SPAN, 512), jnp.float32),
            pltpu.VMEM((CONTEXTS, 8, 128), jnp.float32),
            pltpu.VMEM((OWNERS, 2, 16, 128), jnp.bfloat16),
            pltpu.VMEM((CONTEXTS, 2, 16, 128), jnp.bfloat16),
            pltpu.VMEM((CONTEXTS, 2, 16, 128), jnp.bfloat16),
            pltpu.VMEM((OWNERS, 2, 16, 128), jnp.bfloat16),
            dma((3,)),
            dma((4, PARTS)), dma((4, PARTS)), dma((4, PARTS, 3)), dma((4, PARTS, 3)), dma((5,)), dma((4,)), dma((4,)), dma((4,)),
            dma((4, 4)), dma((4, 4)), dma((4, 4)), dma((4, 4)), dma((4,)), dma((4,)), dma((4,)), dma((4,)), dma, dma,
            dma, dma, dma, dma, dma, dma, dma, dma,
        ],
        compiler_params=pltpu.CompilerParams(collective_id=0, has_side_effects=True, vmem_limit_bytes=60 * 2**20),
        name="layer",
    )(tokens, x_weight, dt_weight.T, bc_weight, conv_x, conv_bc,
      dt_bias.reshape(1, 8), a_rate.reshape(1, 8), d_skip.reshape(1, 8), norm_gain.reshape(1, 512))


def solution(mesh):
    in_specs = (
        P(("context", "tensor"), None),
        P("context", "tensor"),
        P("context", "tensor"),
        P(None, "context", None),
        P(None, "tensor"),
        P(),
        P("tensor"),
        P("tensor"),
        P("tensor"),
        P("tensor"),
    )
    out_specs = P("context", "tensor")
    return jax.shard_map(local, mesh=mesh, in_specs=in_specs, out_specs=out_specs, check_vma=False)
```

```python
import jax
import jax.numpy as jnp
from jax import lax
from jax.experimental import pallas as pl
from jax.experimental.pallas import tpu as pltpu
from jax.sharding import PartitionSpec as P

MESH = pl.DeviceIdType.MESH

HEAD_DIM = 64
STATE = 128
SPAN = 256
CONV = 4
CONTEXTS = 32
OWNERS = 16
PARTS = 2
WIDE = 4096 // PARTS


def place():
    c = lax.axis_index("context")
    t = lax.axis_index("tensor")
    return t // 4, c // 8, t % 4, (c // 2) % 4, c % 2


def device(x, y, z_hi, z_lo, core):
    return ((y % 4) * 8 + (z_lo % 4) * 2 + core, (x % 4) * 4 + z_hi % 4)


def along_z(z, by):
    other = (z + by + 16) % 16
    return other // 4, other % 4


ORDER = ((0, 1, 2, 3), (1, 0, 2, 3), (2, 1, 3, 0), (3, 2, 1, 0))
ONWARD = (None, (1, 1), (-1, -1), (-1, 1))


def pick(index, values):
    out = values[-1]
    for k in range(len(values) - 2, -1, -1):
        out = jnp.where(index == k, values[k], out)
    return out


def layer_kernel(
    tok_ref, w_ref, dt_ref, bc_ref, conv_x_ref, conv_bc_ref, bias_ref, rate_ref, skip_ref, gain_ref,
    out_ref,
    bias, rate, skip, gain, small_sem,
    tok, wb, dts, pre, inner, decays, mine, theirs, leaving, arriving,
    local_sem, tz_s, tz_r, tx_s, tx_r, wz_s, wz_r, bz_s, bz_r,
    wy_s, wy_r, wc_s, wc_r, dz_s, dz_r, dy_s, dy_r, dc_s, dc_r,
    rim_s, rim_r, decay_s, decay_r, state_s, state_r, start_s, start_r,
):
    x, y, z_hi, z_lo, core = place()
    z = z_hi * 4 + z_lo
    t_own = x * 4 + z_hi
    c = lax.axis_index("context")
    t = lax.axis_index("tensor")
    sibling = device(x, y, z_hi, z_lo, 1 - core)

    def describe(src, dst, ssem, rsem, dev):
        return pltpu.make_async_remote_copy(
            src_ref=src, dst_ref=dst, send_sem=ssem, recv_sem=rsem, device_id=dev, device_id_type=MESH
        )

    def send(*args):
        copy = describe(*args)
        copy.start()
        return copy

    def piece(y_at, z_at, core_at):
        return (y_at % 4) * 8 + (z_at % 4) * 2 + core_at

    def x_part(ref, p):
        return ref.at[p, :, pl.ds(0, 512)]

    own = piece(y, z_lo, core)
    group = x * 2 + z_hi // 2
    local = [
        pltpu.make_async_copy(w_ref, x_part(wb, own), local_sem.at[1]),
        pltpu.make_async_copy(bc_ref.at[group], wb.at[own, :, pl.ds(512, 256)], local_sem.at[2]),
        pltpu.make_async_copy(tok_ref, tok.at[t_own], local_sem.at[0]),
    ]
    small = [
        pltpu.make_async_copy(src, dst, small_sem.at[i])
        for i, (src, dst) in enumerate(
            (
                (bias_ref, bias), (rate_ref, rate), (skip_ref, skip), (gain_ref, gain),
            )
        )
    ]
    for copy in local + small:
        copy.start()

    barrier = pltpu.get_barrier_semaphore()
    partners = [device(x, y, z_hi + 1, z_lo, core), device(x, y, z_hi + 3, z_lo, core), sibling]
    for by in (1, 2, 3):
        partners.append(device(x + by, y, z_hi, z_lo, core))
        partners.append(device(x, y + by, z_hi, z_lo, core))
        partners.append(device(x, y, z_hi, z_lo + by, core))
    for by in (1, -1, 2, -2):
        partners.append(device(x, y, *along_z(z, by), core))
    for by in (1, CONTEXTS - 1):
        partners.append(((c + by) % CONTEXTS, t))
    for partner in partners:
        pl.semaphore_signal(barrier, inc=1, device_id=partner, device_id_type=MESH)
    pl.semaphore_wait(barrier, len(partners))

    arrival = [pick(z_lo, [row[j] for row in ORDER]) for j in range(4)]
    guarded = []

    def rows_along_z(z_at, onward, sem, condition):
        to = (z_lo + onward + 4) % 4
        number = pick(to, [pick(z_at, [row.index(k) for k in range(4)]) for row in ORDER])
        block = x_part(wb, piece(y, z_at, core))
        copy = describe(block, block, wz_s.at[sem], wz_r.at[number], device(x, y, z_hi, to, core))

        @pl.when(condition)
        def _():
            copy.start()

        guarded.append((condition, copy))

    for copy in local[:2]:
        copy.wait()
    rows_along_z(z_lo, 1, 0, z_lo < 3)
    rows_along_z(z_lo, -1, 1, z_lo > 0)
    bz = []
    for i, (by, first, count) in enumerate(((1, 0, 128), (-1, 0, 128), (2, 0, 64), (-2, 64, 64))):
        hi, lo = along_z(z, by)
        bz.append(
            send(
                bc_ref.at[x * 2 + hi // 2, pl.ds(first, count)],
                wb.at[own, pl.ds(first, count), pl.ds(512, 256)],
                bz_s.at[i], bz_r.at[i], device(x, y, hi, lo, core),
            )
        )
    dts[core, y, z_lo] = jnp.concatenate(
        [dt_ref[...].astype(jnp.float32), jnp.zeros((8, 128), jnp.float32)], 0
    ).astype(jnp.bfloat16)
    block = dts.at[core, y, z_lo]
    dz = [send(block, block, dz_s.at[by], dz_r.at[by], device(x, y, z_hi, z_lo + by, core)) for by in (1, 2, 3)]

    wy = {}
    wc = {}

    def to_sibling(j, by):
        slot = wb.at[piece(y + by, arrival[j], core)]
        wc[j, by] = send(slot, slot, wc_s.at[j, by], wc_r.at[j, by], sibling)

    def rows_along_y(j):
        slot = wb.at[piece(y, arrival[j], core)]
        wy[j, 0] = send(slot, slot, wy_s.at[j, 0], wy_r.at[j, 0], device(x, y + 1, z_hi, z_lo, core))
        wy[j, 1] = send(slot, slot, wy_s.at[j, 1], wy_r.at[j, 1], device(x, y + 3, z_hi, z_lo, core))
        to_sibling(j, 0)

    def next_rows(j):
        block = x_part(wb, piece(y, arrival[j], core))
        describe(block, block, wz_s.at[0], wz_r.at[j], sibling).wait_recv()
        rows_along_z(arrival[j], jnp.where(z_lo == 1, *ONWARD[j]), 1 + j, (z_lo == 1) | (z_lo == 2))
        rows_along_y(j)

    def relay_along_y(j):
        wy[j, 0].wait_recv()
        half = wb.at[piece(y + 3, arrival[j], core), pl.ds(0, 64)]
        wy[j, 2] = send(half, half, wy_s.at[j, 2], wy_r.at[j, 2], device(x, y + 1, z_hi, z_lo, core))
        wy[j, 1].wait_recv()
        half = wb.at[piece(y + 1, arrival[j], core), pl.ds(64, 64)]
        wy[j, 3] = send(half, half, wy_s.at[j, 3], wy_r.at[j, 3], device(x, y + 3, z_hi, z_lo, core))
        to_sibling(j, 3)
        to_sibling(j, 1)

    def last_along_y(j):
        wy[j, 2].wait_recv()
        wy[j, 3].wait_recv()
        to_sibling(j, 2)

    tx = {}
    tz = {}

    def tokens_along_x(k, hi, part, columns=None):
        slot = tok.at[x * 4 + hi % 4, :, columns_of(part) if columns is None else columns]
        for i, by in enumerate((1, 3, 2)):
            tx[k, part, by] = send(
                slot, slot, tx_s.at[k, part, i], tx_r.at[k, part, i], device(x + by, y, z_hi, z_lo, core)
            )

    def columns_of(part):
        return pl.ds(part * WIDE, WIDE)

    up, down = device(x, y, z_hi + 1, z_lo, core), device(x, y, z_hi + 3, z_lo, core)

    def tokens_along_z():
        for part in range(PARTS):
            block = tok.at[t_own, :, columns_of(part)]
            tz[0, part] = send(block, block, tz_s.at[0, part], tz_r.at[0, part], up)
            tz[1, part] = send(block, block, tz_s.at[1, part], tz_r.at[1, part], down)

    def relay_tokens(part):
        tz[0, part].wait_recv()
        block = tok.at[x * 4 + (z_hi + 3) % 4, :, pl.ds(part * WIDE, WIDE // 2)]
        tz[2, part] = send(block, block, tz_s.at[2, part], tz_r.at[2, part], up)
        tz[1, part].wait_recv()
        block = tok.at[x * 4 + (z_hi + 1) % 4, :, pl.ds(part * WIDE + WIDE // 2, WIDE // 2)]
        tz[3, part] = send(block, block, tz_s.at[3, part], tz_r.at[3, part], down)
        tokens_along_x(1, z_hi + 3, part)
        tokens_along_x(2, z_hi + 1, part)

    def last_tokens(part):
        tz[2, part].wait_recv()
        tz[3, part].wait_recv()
        tokens_along_x(3, z_hi + 2, part)

    rows_along_y(0)
    local[2].wait()
    tokens_along_x(0, z_hi, 0, pl.ds(0, 4096))
    tokens_along_z()
    for copy in dz:
        copy.wait_recv()
    block = dts.at[core, y]
    dy = [
        send(block, block, dy_s.at[by], dy_r.at[by], device(x, y + by, z_hi, z_lo, core)) for by in (1, 2, 3)
    ]
    nearer = jnp.where(z_lo == 0, 1, 0)

    def neighbour_rows(which):
        slot = wb.at[own, :, pl.ds(512, 256)]
        describe(slot, slot, bz_s.at[0], bz_r.at[which], sibling).wait_recv()

    neighbour_rows(nearer)
    next_rows(1)
    neighbour_rows(1 - nearer)
    for copy in bz[2:]:
        copy.wait_recv()
    next_rows(2)
    relay_tokens(0)
    relay_along_y(0)
    for copy in dy:
        copy.wait_recv()
    block = dts.at[core]
    dc = send(block, block, dc_s, dc_r, sibling)
    next_rows(3)
    relay_tokens(1)
    relay_along_y(1)
    last_tokens(0)
    relay_along_y(2)
    relay_along_y(3)
    last_tokens(1)
    for j in range(4):
        last_along_y(j)
    dc.wait_recv()
    for copy in wc.values():
        copy.wait_recv()

    owner = (z_lo == 1) | (z_lo == 2)
    nearest = y * 4 + (z_lo // 2) * 2 + core

    def context_of(o):
        return (o // 4) * 8 + (1 + (o // 2) % 2) * 2 + o % 2

    def to_owners(source, slots, ssem, rsem):
        def one(step, carry):
            o = (nearest + step) % OWNERS
            send(source(o), slots.at[c], ssem, rsem, (context_of(o), t))
            return carry

        @pl.when(~owner)
        def _():
            one(0, 0)

        lax.fori_loop(1, OWNERS, one, 0)

    def several(slots, count, ssem, rsem):
        some = slots.at[pl.ds(0, count)]
        return describe(some, some, ssem, rsem, sibling)

    for copy in small:
        copy.wait()
    both = jnp.zeros((SPAN, 768), jnp.float32)
    dt_raw = jnp.zeros((SPAN, 16), jnp.float32)
    count = CONTEXTS // PARTS
    for part in range(PARTS):
        for (_, at, _), copy in tx.items():
            if at == part:
                copy.wait_recv()
        some = tok[:, :, part * WIDE : (part + 1) * WIDE].reshape(SPAN, WIDE)
        pieces = range(part * count, (part + 1) * count)
        both += jnp.dot(
            some, wb[part * count : (part + 1) * count].reshape(WIDE, 768), preferred_element_type=jnp.float32
        )
        dt_cols = jnp.concatenate([dts[p % 2, p // 8, (p // 2) % 4] for p in pieces], 1)
        dt_raw += lax.dot_general(some, dt_cols, (((1,), (1,)), ((), ())), preferred_element_type=jnp.float32)
    pre[8:] = both.astype(jnp.bfloat16).astype(jnp.float32)
    rim = send(
        pre.at[pl.ds(SPAN, 8)], pre.at[pl.ds(0, 8)], rim_s, rim_r, ((c + 1) % CONTEXTS, t)
    )
    raw = jnp.concatenate([dt_raw, jnp.zeros((SPAN, 112), jnp.float32)], 1).T[:8]
    diagonal = lax.broadcasted_iota(jnp.int32, (8, 8), 0) == lax.broadcasted_iota(jnp.int32, (8, 8), 1)

    def per_head(ref):
        return jnp.sum(jnp.where(diagonal, jnp.broadcast_to(ref[...], (8, 8)), 0.0), axis=1, keepdims=True)

    raw = raw + per_head(bias)
    steps = jnp.maximum(raw, 0.0) + jnp.log1p(jnp.exp(-jnp.abs(raw)))
    upto = lax.broadcasted_iota(jnp.int32, (SPAN, SPAN), 0) <= lax.broadcasted_iota(jnp.int32, (SPAN, SPAN), 1)
    sums = jnp.dot(
        -per_head(rate) * steps, upto.astype(jnp.float32),
        precision=lax.Precision.HIGHEST, preferred_element_type=jnp.float32,
    )
    last = jnp.broadcast_to(sums[:, SPAN - 1 :], (8, SPAN))
    tails = jnp.exp(last - sums) * steps
    columns = jnp.concatenate([sums, tails, jnp.zeros((112, SPAN), jnp.float32)], 0).T
    low_lanes = lax.broadcasted_iota(jnp.int32, (1, 128), 1) < HEAD_DIM
    whole = jnp.exp(last[:, :128])
    decays[c] = jnp.concatenate(
        [jnp.where(low_lanes, whole[2 * b : 2 * b + 1], whole[2 * b + 1 : 2 * b + 2]) for b in range(4)]
        + [jnp.zeros((4, 128), jnp.float32)],
        0,
    )
    to_owners(lambda o: decays.at[c], decays, decay_s, decay_r)

    def spread(first):
        return jnp.concatenate(
            [
                jnp.where(low_lanes, columns[:, first + 2 * b : first + 2 * b + 1], columns[:, first + 2 * b + 1 : first + 2 * b + 2])
                for b in range(4)
            ],
            1,
        )


    x_tap = conv_x_ref[...].astype(jnp.float32)
    bc_tap = conv_bc_ref[group].astype(jnp.float32)

    def convolved(first, width, taps, start, count):
        total = sum(
            taps[k : k + 1] * pre[start + 5 + k : start + 5 + k + count, first : first + width] for k in range(CONV)
        )
        return total / (1.0 + jnp.exp(-total))

    later = (
        convolved(0, 512, x_tap, 8, SPAN - 8),
        convolved(512, 256, bc_tap, 8, SPAN - 8),
    )
    rim.wait_recv()

    @pl.when(c == 0)
    def _():
        pre[:8] = jnp.zeros((8, 768), jnp.float32)

    earlier = (convolved(0, 512, x_tap, 0, 8), convolved(512, 256, bc_tap, 0, 8))
    x_conv, bc_conv = (
        jnp.concatenate(pair, 0).astype(jnp.bfloat16) for pair in zip(earlier, later)
    )
    b_conv, c_conv = bc_conv[:, :STATE], bc_conv[:, STATE:]

    weighted = (x_conv.astype(jnp.float32) * spread(8)).astype(jnp.bfloat16)
    state = lax.dot_general(b_conv, weighted, (((0,), (0,)), ((), ())), preferred_element_type=jnp.float32)
    state = state.astype(jnp.bfloat16)
    for o in range(OWNERS):
        for k in range(2):
            b = 2 * (o % 2) + k
            mine[o, k] = state[16 * (o // 2) : 16 * (o // 2 + 1), 128 * b : 128 * (b + 1)]
    to_owners(lambda o: mine.at[o], theirs, state_s, state_r)
    theirs[c] = mine[nearest]

    scores = lax.dot_general(c_conv, b_conv, (((1,), (1,)), ((), ())), preferred_element_type=jnp.float32)
    upto = lax.broadcasted_iota(jnp.int32, (SPAN, SPAN), 0) >= lax.broadcasted_iota(jnp.int32, (SPAN, SPAN), 1)
    scores = jnp.where(upto, scores, 0.0)

    def within(h):
        gaps = jnp.minimum(columns[:, h : h + 1] - sums[h : h + 1], 0.0)
        mixing = (scores * jnp.exp(gaps) * steps[h : h + 1]).astype(jnp.bfloat16)
        here = x_conv[:, h * HEAD_DIM : (h + 1) * HEAD_DIM]
        return (
            jnp.dot(mixing, here, preferred_element_type=jnp.float32) + skip[:, h : h + 1] * here.astype(jnp.float32)
        )

    for b in range(4):
        inner[:, 128 * b : 128 * (b + 1)] = jnp.concatenate([within(2 * b), within(2 * b + 1)], 1)

    @pl.when(owner)
    def _():
        several(decays, CONTEXTS - 1, decay_s, decay_r).wait_recv()
        several(theirs, CONTEXTS - 1, state_s, state_r).wait_recv()
        carried = jnp.zeros((2, 16, 128), jnp.float32)
        for j in range(CONTEXTS):
            leaving[j] = carried.astype(jnp.bfloat16)
            decay = decays[j, pl.ds(2 * core, 2)].reshape(2, 1, 128)
            carried = decay * carried + theirs[j].astype(jnp.float32)

        def one(step, carry):
            j = (c + step) % CONTEXTS
            send(leaving.at[j], arriving.at[nearest], start_s, start_r, (j, t))
            return carry

        lax.fori_loop(1, CONTEXTS, one, 0)
        arriving[nearest] = leaving[c]

    growth = jnp.exp(spread(0))

    @pl.when(owner)
    def _():
        several(arriving, OWNERS - 1, start_s, start_r).wait_recv()

    @pl.when(~owner)
    def _():
        several(arriving, OWNERS, start_s, start_r).wait_recv()

    start = jnp.concatenate(
        [jnp.concatenate([arriving[2 * i + b // 2, b % 2] for b in range(4)], 1) for i in range(8)], 0
    )
    mixed = inner[...] + growth * jnp.dot(c_conv, start, preferred_element_type=jnp.float32)
    same_head = (
        lax.broadcasted_iota(jnp.int32, (128, 128), 0) // HEAD_DIM == lax.broadcasted_iota(jnp.int32, (128, 128), 1) // HEAD_DIM
    ).astype(jnp.bfloat16)
    for b in range(4):
        part = mixed[:, 128 * b : 128 * (b + 1)]
        square = part * part
        upper = square.astype(jnp.bfloat16)
        lower = (square - upper.astype(jnp.float32)).astype(jnp.bfloat16)
        total = jnp.dot(upper, same_head, preferred_element_type=jnp.float32) + jnp.dot(
            lower, same_head, preferred_element_type=jnp.float32
        )
        scaled = part * lax.rsqrt(total * (1.0 / HEAD_DIM) + 1e-05) * gain[:, 128 * b : 128 * (b + 1)]
        out_ref[:, 128 * b : 128 * (b + 1)] = scaled.astype(jnp.bfloat16)

    for copy in dz + bz + list(tz.values()) + list(tx.values()) + list(wy.values()) + list(wc.values()) + dy + [dc, rim]:
        copy.wait_send()
    for condition, copy in guarded:

        @pl.when(condition)
        def _(copy=copy):
            copy.wait_send()


    @pl.when(owner)
    def _():
        several(decays, OWNERS - 1, decay_s, decay_r).wait_send()
        several(mine, OWNERS - 1, state_s, state_r).wait_send()
        several(leaving, CONTEXTS - 1, start_s, start_r).wait_send()

    @pl.when(~owner)
    def _():
        several(decays, OWNERS, decay_s, decay_r).wait_send()
        several(mine, OWNERS, state_s, state_r).wait_send()


def local(
    tokens, x_weight, dt_weight, bc_weight, conv_x, conv_bc, dt_bias, a_rate, d_skip, norm_gain
):
    dma = pltpu.SemaphoreType.DMA
    in_vmem = pl.BlockSpec(memory_space=pltpu.VMEM)
    anywhere = pl.BlockSpec(memory_space=pltpu.HBM)
    return pl.pallas_call(
        layer_kernel,
        out_shape=jax.ShapeDtypeStruct((SPAN, 512), jnp.bfloat16),
        in_specs=[anywhere, anywhere, in_vmem, anywhere, in_vmem, in_vmem] + [anywhere] * 4,
        out_specs=in_vmem,
        scratch_shapes=[
            pltpu.VMEM((1, 8), jnp.float32),
            pltpu.VMEM((1, 8), jnp.float32),
            pltpu.VMEM((1, 8), jnp.float32),
            pltpu.VMEM((1, 512), jnp.float32),
            dma((4,)),
            pltpu.VMEM((16, 16, 4096), jnp.bfloat16),
            pltpu.VMEM((32, 128, 768), jnp.bfloat16),
            pltpu.VMEM((2, 4, 4, 16, 128), jnp.bfloat16),
            pltpu.VMEM((8 + SPAN, 768), jnp.float32),
            pltpu.VMEM((SPAN, 512), jnp.float32),
            pltpu.VMEM((CONTEXTS, 8, 128), jnp.float32),
            pltpu.VMEM((OWNERS, 2, 16, 128), jnp.bfloat16),
            pltpu.VMEM((CONTEXTS, 2, 16, 128), jnp.bfloat16),
            pltpu.VMEM((CONTEXTS, 2, 16, 128), jnp.bfloat16),
            pltpu.VMEM((OWNERS, 2, 16, 128), jnp.bfloat16),
            dma((3,)),
            dma((4, PARTS)), dma((4, PARTS)), dma((4, PARTS, 3)), dma((4, PARTS, 3)), dma((5,)), dma((4,)), dma((4,)), dma((4,)),
            dma((4, 4)), dma((4, 4)), dma((4, 4)), dma((4, 4)), dma((4,)), dma((4,)), dma((4,)), dma((4,)), dma, dma,
            dma, dma, dma, dma, dma, dma, dma, dma,
        ],
        compiler_params=pltpu.CompilerParams(collective_id=0, has_side_effects=True, vmem_limit_bytes=60 * 2**20),
        name="layer",
    )(tokens, x_weight, dt_weight.T, bc_weight, conv_x, conv_bc,
      dt_bias.reshape(1, 8), a_rate.reshape(1, 8), d_skip.reshape(1, 8), norm_gain.reshape(1, 512))


def solution(mesh):
    in_specs = (
        P(("context", "tensor"), None),
        P("context", "tensor"),
        P("context", "tensor"),
        P(None, "context", None),
        P(None, "tensor"),
        P(),
        P("tensor"),
        P("tensor"),
        P("tensor"),
        P("tensor"),
    )
    out_specs = P("context", "tensor")
    return jax.shard_map(local, mesh=mesh, in_specs=in_specs, out_specs=out_specs, check_vma=False)
```
